256 devices in a mesh: seq: 8 (over y_lo, x), expert: 32 (over z, y_hi, core).
Axes of the slice: x: 4, y: 4 (y_hi: 2, y_lo: 2; y = y_hi * 2 + y_lo), z: 8, core: 2. Of those that a mesh axis runs over, the one named last changes fastest.
Arguments:
- tokens: bfloat16 [32768, 4096], P(('seq', 'expert')), may hold values from -40 to 40
- slot_keys: bfloat16 [64, 4096], P('expert'), may hold values from -12 to 12
- w_in: bfloat16 [32, 4096, 2048], P('expert', None, 'seq'), may hold values from -0.09375 to 0.09375
- w_out: bfloat16 [32, 2048, 4096], P('expert', 'seq'), may hold values from -0.125 to 0.125
- cotangent: bfloat16 [32768, 4096], P(('seq', 'expert')), may hold values from -6 to 6
Outputs:
- layer_out: bfloat16 [32768, 4096], P(('seq', 'expert'))
- token_grad: bfloat16 [32768, 4096], P(('seq', 'expert'))
- key_grad: float32 [64, 4096], P('expert')
- w_in_grad: bfloat16 [32, 4096, 2048], P('expert', None, 'seq')
- w_out_grad: bfloat16 [32, 2048, 4096], P('expert', 'seq')
The draws below stay inside these ranges and needn't reach their ends.
All inputs are finite; a program needn't handle non-finite values.
Results may differ from the reference program's by a relative error of at most 0.03.
Values may be sent and summed in bfloat16 or wider, within the bound.
No kernel may reach another device: no remote copies, remote signals or barrier semaphores. Data moves between devices by JAX's collectives and lax.ppermute only.
A program may use at most 64 MiB of HBM per device.

```python
import math
import jax
import jax.numpy as jnp
from jax import lax

D = 4096
FFN = 2048
SLOTS = 2
EXPERTS = 32
TOKENS = 32768


def draw_tokens(key, part):
    key = jax.random.fold_in(key, 7)
    key_noise, key_scale = jax.random.split(key, 2)
    position = jnp.arange(TOKENS, dtype=jnp.float32) / TOKENS
    rough_scale = jnp.exp(jax.random.uniform(key_scale, (TOKENS, 1), jnp.float32, 0.0, math.log(2.0)))
    row_scale = rough_scale * (1.0 + position)[:, None]
    result = jax.random.normal(key_noise, (TOKENS, D), jnp.float32) * row_scale
    return jnp.clip(result, -40.0, 40.0).astype(jnp.bfloat16)


def draw_slot_keys(key, part):
    key = jax.random.fold_in(key, 13)
    key_main, key_scale = jax.random.split(key, 2)
    slot_count = EXPERTS * SLOTS
    row_scale = jnp.exp(jax.random.uniform(key_scale, (slot_count, 1), jnp.float32, math.log(0.8), math.log(1.25)))
    result = jax.random.normal(key_main, (slot_count, D), jnp.float32) * row_scale * (0.5 / math.sqrt(D))
    return jnp.clip(result, -12.0, 12.0).astype(jnp.bfloat16)


def shard_levels(own_key, extent, cuts, low, top_value):
    level = 1.0
    for dim, blocks in cuts:
        heights = jax.random.uniform(jax.random.fold_in(jax.random.fold_in(own_key, 6), dim), (blocks,), jnp.float32, low / len(cuts), top_value / len(cuts))
        level = level * jnp.repeat(jnp.exp(heights), extent[dim] // blocks).reshape((-1,) + (1,) * (len(extent) - 1 - dim))
    return level


def normal_values(rng, shape, deviation, bound, shards=(), held_as=jnp.bfloat16):
    entries = deviation * jax.random.normal(rng, shape, jnp.float32)
    if shards:
        entries = entries * shard_levels(rng, shape, shards, -0.22, 0.18)
    return jnp.clip(entries, -bound, bound).astype(held_as)


def setup_inputs(seed: int = 0) -> dict:
    splits = jax.random.split(jax.random.key(seed), 6)
    return {
        "tokens": draw_tokens(jax.random.fold_in(splits[5], 71), 0),
        "slot_keys": draw_slot_keys(jax.random.fold_in(splits[5], 71), 0),
        "w_in": normal_values(splits[2], (EXPERTS, D, FFN), D ** -0.5, 0.09375, ((0, 32), (2, 8))),
        "w_out": normal_values(splits[3], (EXPERTS, FFN, D), FFN ** -0.5, 0.125, ((0, 32), (1, 8))),
        "cotangent": normal_values(splits[4], (TOKENS, D), 1.0, 6.0, ((0, 256),)),
    }


def gelu_tanh(values):
    return jax.nn.gelu(values, approximate=True)

def expert_forward(parts):
    slot_one, first_w, second_w = parts
    pre_one = jnp.dot(slot_one, first_w, preferred_element_type=jnp.float32)
    act_one = gelu_tanh(pre_one).astype(jnp.bfloat16)
    out_one = jnp.dot(act_one, second_w, preferred_element_type=jnp.float32)
    return (pre_one, act_one, out_one)

def expert_backward(parts):
    slot_one, first_w, second_w, pre_one, act_one, grad_one = parts
    second_grad = jnp.dot(act_one.T, grad_one, preferred_element_type=jnp.float32)
    act_grad = jnp.dot(grad_one, second_w.T, preferred_element_type=jnp.float32)
    _, pullback = jax.vjp(gelu_tanh, pre_one)
    pre_grad = pullback(act_grad)[0].astype(jnp.bfloat16)
    first_grad = jnp.dot(slot_one.T, pre_grad, preferred_element_type=jnp.float32)
    slot_back = jnp.dot(pre_grad, first_w.T, preferred_element_type=jnp.float32)
    return (first_grad.astype(jnp.bfloat16), second_grad.astype(jnp.bfloat16), slot_back)

def reference(tokens, slot_keys, w_in, w_out, cotangent):
    logits = jnp.dot(slot_keys, tokens.T, preferred_element_type=jnp.float32)
    row_peak = lax.optimization_barrier(jnp.max(logits, axis=1, keepdims=True))
    row_exp = jnp.exp(logits - row_peak)
    dispatch = (row_exp / lax.optimization_barrier(jnp.sum(row_exp, axis=1, keepdims=True))).astype(jnp.bfloat16)
    slot_sum = jnp.dot(dispatch, tokens, preferred_element_type=jnp.float32)
    slot_in = slot_sum.astype(jnp.bfloat16).reshape(EXPERTS, SLOTS, D)
    pre_act, hidden_act, slot_out = lax.map(expert_forward, (slot_in, w_in, w_out))
    slot_out = slot_out.reshape(EXPERTS * SLOTS, D).astype(jnp.bfloat16)
    col_peak = lax.optimization_barrier(jnp.max(logits, axis=0, keepdims=True))
    col_exp = jnp.exp(logits - col_peak)
    combine = (col_exp / lax.optimization_barrier(jnp.sum(col_exp, axis=0, keepdims=True))).astype(jnp.bfloat16)
    layer_out = jnp.dot(combine.T, slot_out, preferred_element_type=jnp.float32).astype(jnp.bfloat16)
    combine_dot = jnp.dot(slot_out, cotangent.T, preferred_element_type=jnp.float32)
    combine_wide = combine.astype(jnp.float32)
    combine_grad = combine_wide * (combine_dot - lax.optimization_barrier(jnp.sum(combine_wide * combine_dot, axis=0, keepdims=True)))
    out_grad = jnp.dot(combine, cotangent, preferred_element_type=jnp.float32).astype(jnp.bfloat16)
    out_grad = out_grad.reshape(EXPERTS, SLOTS, D)
    w_in_grad, w_out_grad, slot_back = lax.map(expert_backward, (slot_in, w_in, w_out, pre_act, hidden_act, out_grad))
    slot_grad = slot_back.reshape(EXPERTS * SLOTS, D).astype(jnp.bfloat16)
    pick_grad = jnp.dot(slot_grad, tokens.T, preferred_element_type=jnp.float32)
    dispatch_wide = dispatch.astype(jnp.float32)
    crossing = lax.optimization_barrier(jnp.sum(dispatch_wide * pick_grad, axis=1, keepdims=True))
    logit_grad = (dispatch_wide * (pick_grad - crossing) + combine_grad).astype(jnp.bfloat16)
    token_grad = jnp.dot(dispatch.T, slot_grad, preferred_element_type=jnp.float32)
    token_grad = (token_grad + jnp.dot(logit_grad.T, slot_keys, preferred_element_type=jnp.float32)).astype(jnp.bfloat16)
    key_grad = jnp.dot(logit_grad, tokens, preferred_element_type=jnp.float32)
    return (layer_out, token_grad, key_grad, w_in_grad, w_out_grad)
```

```python
import jax
import jax.numpy as jnp
from jax import lax
from jax.sharding import PartitionSpec as P

F32 = jnp.float32
BF16 = jnp.bfloat16


def gelu_tanh(values):
    return jax.nn.gelu(values, approximate=True)


def split_f32(values):
    high = lax.reduce_precision(values, 8, 7)
    rest = values - high
    middle = lax.reduce_precision(rest, 8, 7)
    return [high.astype(BF16), middle.astype(BF16), (rest - middle).astype(BF16)]


def with_stats(values, stats):
    pieces = [p[..., None] for s in stats for p in split_f32(s)]
    lead = values.shape[:-1]
    pad = jnp.zeros(lead + (128 - len(pieces),), BF16)
    return jnp.concatenate([values.astype(BF16)] + pieces + [pad], axis=-1)


def read_stats(message, width, count):
    cols = message[..., width : width + 3 * count].astype(F32)
    return [cols[..., 3 * i] + cols[..., 3 * i + 1] + cols[..., 3 * i + 2] for i in range(count)]


def body(tokens, slot_keys, w_in, w_out, cotangent):
    width = tokens.shape[1]
    seq = lax.axis_size("seq")
    experts = lax.axis_size("expert")
    half = experts // 2
    same_core = [[2 * i + c for i in range(half)] for c in range(2)]
    partner = [(i, i ^ 1) for i in range(experts)]

    def swap(values):
        return lax.ppermute(values, "expert", partner)

    def exchange(values):
        return lax.all_to_all(values, "expert", 0, 0, tiled=True, axis_index_groups=same_core)

    def gather_half(values):
        return exchange(jnp.broadcast_to(values[None], (half,) + values.shape))

    def gather_seq(values):
        return lax.all_to_all(
            jnp.broadcast_to(values[None], (seq,) + values.shape), "seq", 0, 0, tiled=True
        )

    rows = slot_keys.shape[0]
    own = half * rows
    keys_own = gather_half(slot_keys).reshape(own, width)
    keys_all = jnp.concatenate([keys_own, swap(keys_own)], axis=0)

    logits = jnp.einsum("jd,td->jt", keys_all, tokens, preferred_element_type=F32)
    col_peak = jnp.max(logits, axis=0, keepdims=True)
    col_exp = jnp.exp(logits - col_peak)
    combine = (col_exp / jnp.sum(col_exp, axis=0, keepdims=True)).astype(BF16)
    combine_wide = combine.astype(F32)
    peak = jnp.max(logits, axis=1)
    row_exp = jnp.exp(logits - peak[:, None])
    total = jnp.sum(row_exp, axis=1)
    part_in = jnp.dot(row_exp.astype(BF16), tokens, preferred_element_type=F32)
    part_grad = jnp.dot(combine, cotangent, preferred_element_type=F32)

    def merge(first, second, peaks, totals):
        top = jnp.max(peaks, axis=0)
        scale = jnp.exp(peaks - top)
        return (
            jnp.sum(first.astype(F32) * scale[..., None], axis=0),
            jnp.sum(second.astype(F32), axis=0),
            top,
            jnp.sum(totals * scale, axis=0),
        )

    def merge_messages(message):
        peaks, totals = read_stats(message, 2 * width, 2)
        return merge(message[..., :width], message[..., width : 2 * width], peaks, totals)

    def pack(first, second, peaks, totals):
        return with_stats(jnp.concatenate([first, second], axis=-1), [peaks, totals])

    other = swap(pack(part_in[own:], part_grad[own:], peak[own:], total[own:]))
    other_peak, other_total = read_stats(other, 2 * width, 2)
    merged = merge(
        jnp.stack([part_in[:own], other[:, :width].astype(F32)]),
        jnp.stack([part_grad[:own], other[:, width : 2 * width].astype(F32)]),
        jnp.stack([peak[:own], other_peak]),
        jnp.stack([total[:own], other_total]),
    )
    message = exchange(pack(*merged).reshape(half, rows, -1))
    message = gather_seq(pack(*merge_messages(message)))
    slot_sum, out_sum, slot_peak, slot_total = merge_messages(message)
    slot_sum = slot_sum / slot_total[:, None]
    slot_in = slot_sum.astype(BF16)
    out_grad = out_sum.astype(BF16)

    w_first, w_second = w_in[0], w_out[0]
    pre_act = jnp.dot(slot_in, w_first, preferred_element_type=F32)
    hidden_act = gelu_tanh(pre_act).astype(BF16)
    out_part = jnp.dot(hidden_act, w_second, preferred_element_type=F32)
    act_grad = jnp.einsum("sd,fd->sf", out_grad, w_second, preferred_element_type=F32)
    _, pullback = jax.vjp(gelu_tanh, pre_act)
    pre_grad = pullback(act_grad)[0].astype(BF16)
    slot_part = jnp.einsum("sf,df->sd", pre_grad, w_first, preferred_element_type=F32)
    w_out_grad = jnp.einsum(
        "sf,sd->fd", hidden_act, out_grad, preferred_element_type=F32
    ).astype(BF16)[None]
    w_in_grad = jnp.einsum(
        "sd,sf->df", slot_in, pre_grad, preferred_element_type=F32
    ).astype(BF16)[None]

    parts = jnp.concatenate([out_part, slot_part], axis=0).astype(BF16)
    sums = jnp.sum(gather_seq(parts).astype(F32), axis=0).astype(BF16)
    crossing_own = jnp.sum(sums[rows:].astype(F32) * slot_sum, axis=1)
    message = with_stats(
        sums,
        [
            jnp.concatenate([slot_peak, crossing_own]),
            jnp.concatenate([slot_total, jnp.zeros_like(crossing_own)]),
        ],
    )
    message = gather_half(message)
    message = jnp.concatenate([message, swap(message)], axis=0)
    stat_one, stat_two = read_stats(message, width, 2)
    slot_out = message[:, :rows, :width].reshape(2 * own, width)
    slot_grad = message[:, rows:, :width].reshape(2 * own, width)
    peak_all = stat_one[:, :rows].reshape(2 * own, 1)
    crossing = stat_one[:, rows:].reshape(2 * own, 1)
    total_all = stat_two[:, :rows].reshape(2 * own, 1)

    dispatch = (jnp.exp(logits - peak_all) / total_all).astype(BF16)
    layer_out = jnp.einsum("jt,jd->td", combine, slot_out, preferred_element_type=F32).astype(BF16)
    combine_dot = jnp.einsum("jd,td->jt", slot_out, cotangent, preferred_element_type=F32)
    combine_grad = combine_wide * (
        combine_dot - jnp.sum(combine_wide * combine_dot, axis=0, keepdims=True)
    )
    pick_grad = jnp.einsum("jd,td->jt", slot_grad, tokens, preferred_element_type=F32)
    logit_grad = (dispatch.astype(F32) * (pick_grad - crossing) + combine_grad).astype(BF16)
    key_part = jnp.dot(logit_grad, tokens, preferred_element_type=F32)
    token_grad = jnp.einsum(
        "jt,jd->td",
        jnp.concatenate([dispatch, logit_grad], axis=0),
        jnp.concatenate([slot_grad, keys_all], axis=0),
        preferred_element_type=F32,
    ).astype(BF16)

    key_sum = key_part[:own] + swap(key_part[own:].astype(BF16)).astype(F32)
    key_sum = exchange(key_sum.astype(BF16).reshape(half, rows, width))
    key_sum = jnp.sum(key_sum.astype(F32), axis=0)
    key_grad = jnp.sum(gather_seq(key_sum), axis=0)
    return (layer_out, token_grad, key_grad, w_in_grad, w_out_grad)


def solution(mesh):
    in_specs = (
        P(("seq", "expert"), None),
        P("expert", None),
        P("expert", None, "seq"),
        P("expert", "seq", None),
        P(("seq", "expert"), None),
    )
    out_specs = (
        P(("seq", "expert"), None),
        P(("seq", "expert"), None),
        P("expert", None),
        P("expert", None, "seq"),
        P("expert", "seq", None),
    )
    return jax.shard_map(body, mesh=mesh, in_specs=in_specs, out_specs=out_specs, check_vma=False)
```

```python
import math

import jax
import jax.numpy as jnp
from jax import lax
from jax.experimental import pallas as pl
from jax.experimental.pallas import tpu as pltpu
from jax.sharding import PartitionSpec as P

F32 = jnp.float32
BF16 = jnp.bfloat16
LANES = 128
ROOT = math.sqrt(2.0 / math.pi)
CUBE = 0.044715


def dot(a, b, a_dim, b_dim):
    return lax.dot_general(a, b, (((a_dim,), (b_dim,)), ((), ())), preferred_element_type=F32)


def pieces(values):
    high = values.astype(BF16).astype(F32)
    rest = values - high
    middle = rest.astype(BF16).astype(F32)
    return [high, middle, rest - middle]


def stat_block(stats):
    lane = lax.broadcasted_iota(jnp.int32, (stats[0].shape[0], LANES), 1)
    block = jnp.zeros(lane.shape, F32)
    for i, piece in enumerate([p for s in stats for p in pieces(s)]):
        block = jnp.where(lane == i, piece, block)
    return block


def read_stat(block, i):
    cols = [block[..., k : k + 1].astype(F32) for k in range(3 * i, 3 * i + 3)]
    return cols[0] + cols[1] + cols[2]


def copies_kernel(values, out):
    for i in range(out.shape[0]):
        out[i] = values[...]


def dispatch_kernel(keys_own, keys_other, tokens, cotangent, keys_all, logits, combine, keep, send):
    width = tokens.shape[1]
    own = keep.shape[0]
    keys_all[:own] = keys_own[...].reshape(own, width)
    keys_all[own:] = keys_other[...].reshape(own, width)
    value = dot(keys_all[...], tokens[...], 1, 1)
    logits[...] = value
    col_exp = jnp.exp(value - jnp.max(value, axis=0, keepdims=True))
    weights = (col_exp / jnp.sum(col_exp, axis=0, keepdims=True)).astype(BF16)
    combine[...] = weights
    peak = jnp.max(value, axis=1, keepdims=True)
    row_exp = jnp.exp(value - peak)
    total = jnp.sum(row_exp, axis=1, keepdims=True)
    part = dot(row_exp.astype(BF16), tokens[...], 1, 0)
    keep[:, :width] = part[:own]
    send[:, :width] = part[own:].astype(BF16)
    part = dot(weights, cotangent[...], 1, 0)
    keep[:, width : 2 * width] = part[:own]
    send[:, width : 2 * width] = part[own:].astype(BF16)
    send[:, 2 * width :] = stat_block([peak[own:], total[own:]]).astype(BF16)
    lane = lax.broadcasted_iota(jnp.int32, (own, LANES), 1)
    keep[:, 2 * width :] = jnp.where(lane == 0, peak[:own], total[:own])


def pair_kernel(keep, other, out):
    width = (keep.shape[1] - LANES) // 2
    rows = keep.shape[0]
    stats = other[:, 2 * width :]
    peaks = [keep[:, 2 * width : 2 * width + 1], read_stat(stats, 0)]
    totals = [keep[:, 2 * width + 1 : 2 * width + 2], read_stat(stats, 1)]
    top = jnp.maximum(*peaks)
    scales = [jnp.exp(p - top) for p in peaks]
    first = keep[:, :width] * scales[0] + other[:, :width].astype(F32) * scales[1]
    out[:, :, :width] = first.astype(BF16).reshape(out.shape[0], out.shape[1], width)
    second = keep[:, width : 2 * width] + other[:, width : 2 * width].astype(F32)
    out[:, :, width : 2 * width] = second.astype(BF16).reshape(out.shape[0], out.shape[1], width)
    block = stat_block([top, totals[0] * scales[0] + totals[1] * scales[1]])
    out[:, :, 2 * width :] = block.astype(BF16).reshape(out.shape[0], out.shape[1], LANES)


def merge(message):
    width = (message.shape[2] - LANES) // 2
    stats = message[:, :, 2 * width :]
    peaks, totals = read_stat(stats, 0), read_stat(stats, 1)
    top = jnp.max(peaks, axis=0, keepdims=True)
    scales = jnp.exp(peaks - top)
    total = jnp.sum(totals * scales, axis=0)
    first = message[0, :, :width].astype(F32) * scales[0]
    for p in range(1, message.shape[0]):
        first += message[p, :, :width].astype(F32) * scales[p]
    second = message[0, :, width : 2 * width].astype(F32)
    for p in range(1, message.shape[0]):
        second += message[p, :, width : 2 * width].astype(F32)
    return first, second, top[0], total


def merge_kernel(message, out):
    width = (message.shape[2] - LANES) // 2
    first, second, top, total = merge(message)
    first, second = first.astype(BF16), second.astype(BF16)
    block = stat_block([top, total]).astype(BF16)
    for i in range(out.shape[0]):
        out[i, :, :width] = first
        out[i, :, width : 2 * width] = second
        out[i, :, 2 * width :] = block


def expert_kernel(
    message, w_in, w_out, parts, sums, stats, slot_in_out, out_grad_out, hidden_out, pre_grad_out
):
    width = sums.shape[1]
    first, second, top, total = merge(message)
    slot_sum = first / total
    sums[...] = slot_sum
    lane = lax.broadcasted_iota(jnp.int32, stats.shape, 1)
    stats[...] = jnp.where(lane == 0, top, total)
    slot_in = slot_sum.astype(BF16)
    out_grad = second.astype(BF16)
    slot_in_out[...] = slot_in
    out_grad_out[...] = out_grad
    pre_act = dot(slot_in, w_in[...], 1, 0)
    tanh = jnp.tanh(ROOT * (pre_act + CUBE * (pre_act * pre_act * pre_act)))
    hidden = (pre_act * (0.5 * (1.0 + tanh))).astype(BF16)
    hidden_out[...] = hidden
    act_grad = dot(out_grad, w_out[...], 1, 1)
    slope = 0.5 * (1.0 + tanh) + 0.5 * pre_act * (1.0 - tanh * tanh) * (
        ROOT * (1.0 + 3.0 * CUBE * (pre_act * pre_act))
    )
    pre_grad = (act_grad * slope).astype(BF16)
    pre_grad_out[...] = pre_grad
    out_part = dot(hidden, w_out[...], 1, 0).astype(BF16)
    slot_part = dot(pre_grad, w_in[...], 1, 1).astype(BF16)
    for i in range(parts.shape[0]):
        parts[i, :, :width] = out_part
        parts[i, :, width:] = slot_part


def outs_kernel(parts, sums, stats, out):
    width = sums.shape[1]
    total = parts[0].astype(F32)
    for p in range(1, parts.shape[0]):
        total += parts[p].astype(F32)
    values = total.astype(BF16)
    crossing = jnp.sum(values[:, width:].astype(F32) * sums[...], axis=1, keepdims=True)
    block = stat_block([stats[:, 0:1], stats[:, 1:2], crossing]).astype(BF16)
    for i in range(out.shape[0]):
        out[i, :, : 2 * width] = values
        out[i, :, 2 * width :] = block


def token_kernel(
    outs_own, outs_other, tokens, cotangent, logits, combine,
    slot_out, slot_grad, dispatch_out, logit_grad_out, keep, send,
):
    width = tokens.shape[1]
    own = keep.shape[0]
    blocks = []
    for i, outs in enumerate((outs_own, outs_other)):
        rows = pl.ds(i * own, own)
        slot_out[rows] = outs[:, :, :width].reshape(own, width)
        slot_grad[rows] = outs[:, :, width : 2 * width].reshape(own, width)
        blocks.append(outs[:, :, 2 * width :].reshape(own, LANES).astype(F32))
    block = jnp.concatenate(blocks, axis=0)
    peak, total, crossing = (read_stat(block, i) for i in range(3))
    dispatch = (jnp.exp(logits[...] - peak) / total).astype(BF16)
    dispatch_out[...] = dispatch
    weights = combine[...].astype(F32)
    combine_dot = dot(slot_out[...], cotangent[...], 1, 1)
    combine_grad = weights * (combine_dot - jnp.sum(weights * combine_dot, axis=0, keepdims=True))
    pick_grad = dot(slot_grad[...], tokens[...], 1, 1)
    logit_grad = (dispatch.astype(F32) * (pick_grad - crossing) + combine_grad).astype(BF16)
    logit_grad_out[...] = logit_grad
    part = dot(logit_grad, tokens[...], 1, 0)
    keep[...] = part[:own]
    send[...] = part[own:].astype(BF16)


def key_pair_kernel(keep, other, out):
    out[...] = (keep[...] + other[...].astype(F32)).astype(BF16).reshape(out.shape)


def key_merge_kernel(message, out):
    total = message[0].astype(F32)
    for p in range(1, message.shape[0]):
        total += message[p].astype(F32)
    for i in range(out.shape[0]):
        out[i] = total.astype(out.dtype)


def key_sum_kernel(message, out):
    total = message[0].astype(F32)
    for p in range(1, message.shape[0]):
        total += message[p].astype(F32)
    out[...] = total


def call(kernel, outs, *args):
    whole = pl.BlockSpec(memory_space=pltpu.VMEM)
    return pl.pallas_call(
        kernel,
        out_shape=[pltpu.VMEM(shape, dtype) for shape, dtype in outs],
        in_specs=[whole] * len(args),
        out_specs=[whole] * len(outs),
        compiler_params=pltpu.CompilerParams(vmem_limit_bytes=24 * 1024 * 1024),
    )(*args)


def body(tokens, slot_keys, w_in, w_out, cotangent):
    count, width = tokens.shape
    hidden_units = w_in.shape[2]
    seq = lax.axis_size("seq")
    experts = lax.axis_size("expert")
    rows = slot_keys.shape[0]
    half = experts // 2
    own = half * rows
    slots = 2 * own
    long = 2 * width + LANES
    same_core = [[2 * i + c for i in range(half)] for c in range(2)]
    partner = [(i, i ^ 1) for i in range(experts)]

    def swap(values):
        return lax.ppermute(values, "expert", partner)

    def exchange(values):
        return lax.all_to_all(values, "expert", 0, 0, tiled=True, axis_index_groups=same_core)

    def exchange_seq(values):
        return lax.all_to_all(values, "seq", 0, 0, tiled=True)

    (message,) = call(copies_kernel, [((half, rows, width), BF16)], slot_keys)
    keys_own = exchange(message)
    keys_all, logits, combine, keep, send = call(
        dispatch_kernel,
        [
            ((slots, width), BF16),
            ((slots, count), F32),
            ((slots, count), BF16),
            ((own, long), F32),
            ((own, long), BF16),
        ],
        keys_own, swap(keys_own), tokens, cotangent,
    )
    (message,) = call(pair_kernel, [((half, rows, long), BF16)], keep, swap(send))
    (message,) = call(merge_kernel, [((seq, rows, long), BF16)], exchange(message))
    parts, sums, stats, slot_in, out_grad, hidden, pre_grad = call(
        expert_kernel,
        [
            ((seq, rows, 2 * width), BF16),
            ((rows, width), F32),
            ((rows, LANES), F32),
            ((rows, width), BF16),
            ((rows, width), BF16),
            ((rows, hidden_units), BF16),
            ((rows, hidden_units), BF16),
        ],
        exchange_seq(message), w_in[0], w_out[0],
    )
    (message,) = call(
        outs_kernel, [((half, rows, long), BF16)], exchange_seq(parts), sums, stats
    )
    outs = exchange(message)
    slot_out, slot_grad, dispatch, logit_grad, keep, send = call(
        token_kernel,
        [
            ((slots, width), BF16),
            ((slots, width), BF16),
            ((slots, count), BF16),
            ((slots, count), BF16),
            ((own, width), F32),
            ((own, width), BF16),
        ],
        outs, swap(outs), tokens, cotangent, logits, combine,
    )
    (message,) = call(key_pair_kernel, [((half, rows, width), BF16)], keep, swap(send))
    (message,) = call(key_merge_kernel, [((seq, rows, width), F32)], exchange(message))
    (key_grad,) = call(key_sum_kernel, [((rows, width), F32)], exchange_seq(message))

    w_out_grad = dot(hidden, out_grad, 0, 0).astype(BF16)[None]
    w_in_grad = dot(slot_in, pre_grad, 0, 0).astype(BF16)[None]
    layer_out = dot(combine, slot_out, 0, 0).astype(BF16)
    token_grad = dot(
        jnp.concatenate([dispatch, logit_grad], axis=0),
        jnp.concatenate([slot_grad, keys_all], axis=0),
        0,
        0,
    ).astype(BF16)
    return (layer_out, token_grad, key_grad, w_in_grad, w_out_grad)


def solution(mesh):
    in_specs = (
        P(("seq", "expert"), None),
        P("expert", None),
        P("expert", None, "seq"),
        P("expert", "seq", None),
        P(("seq", "expert"), None),
    )
    out_specs = (
        P(("seq", "expert"), None),
        P(("seq", "expert"), None),
        P("expert", None),
        P("expert", None, "seq"),
        P("expert", "seq", None),
    )
    return jax.shard_map(body, mesh=mesh, in_specs=in_specs, out_specs=out_specs, check_vma=False)
```

```python
import math

import jax
import jax.numpy as jnp
from jax import lax
from jax.experimental import pallas as pl
from jax.experimental.pallas import tpu as pltpu
from jax.sharding import PartitionSpec as P

F32 = jnp.float32
BF16 = jnp.bfloat16
TAIL = 256
ROOT = math.sqrt(2.0 / math.pi)
CUBE = 0.044715


def dot(a, b, a_dim, b_dim):
    return lax.dot_general(a, b, (((a_dim,), (b_dim,)), ((), ())), preferred_element_type=F32)


def pieces(values):
    high = values.astype(BF16).astype(F32)
    rest = values - high
    middle = rest.astype(BF16).astype(F32)
    return [high, middle, rest - middle]


def stat_block(stats):
    lane = lax.broadcasted_iota(jnp.int32, (stats[0].shape[0], TAIL), 1)
    block = jnp.zeros(lane.shape, F32)
    for i, piece in enumerate([p for s in stats for p in pieces(s)]):
        block = jnp.where(lane == i, piece, block)
    return block


def read_stat(block, i):
    cols = [block[..., k : k + 1].astype(F32) for k in range(3 * i, 3 * i + 3)]
    return cols[0] + cols[1] + cols[2]


def copies_kernel(values, out):
    for i in range(out.shape[0]):
        out[i] = values[...]


def logit_kernel(message, tokens, tokens_other, keys, logits, columns):
    own, width = keys.shape
    keys[...] = message[...].reshape(own, width)
    value = jnp.concatenate(
        [dot(keys[...], tokens[...], 1, 1), dot(keys[...], tokens_other[...], 1, 1)], axis=1
    )
    logits[...] = value
    peak = jnp.max(value, axis=0, keepdims=True)
    columns[0:1, :] = peak
    columns[1:2, :] = jnp.sum(jnp.exp(value - peak), axis=0, keepdims=True)


def dispatch_kernel(logits, tokens, tokens_other, sums, stats):
    count = tokens.shape[0]
    value = logits[...]
    peak = jnp.max(value, axis=1, keepdims=True)
    weights = jnp.exp(value - peak)
    total = jnp.sum(weights, axis=1, keepdims=True)
    weights = weights.astype(BF16)
    part = dot(weights[:, :count], tokens[...], 1, 0)
    part += dot(weights[:, count:], tokens_other[...], 1, 0)
    sums[...] = part.astype(BF16).reshape(sums.shape)
    stats[...] = stat_block([peak, total]).astype(BF16).reshape(stats.shape)


def turn(columns, count):
    return jnp.concatenate([columns[:, count:], columns[:, :count]], axis=1)


def combine_kernel(logits, columns, columns_other, cotangent, cotangent_other, sums, stats, combine, out):
    count, width = cotangent.shape
    other = turn(columns_other[...], count)
    here = columns[...]
    peak = jnp.maximum(here[0:1], other[0:1])
    total = here[1:2] * jnp.exp(here[0:1] - peak) + other[1:2] * jnp.exp(other[0:1] - peak)
    weights = (jnp.exp(logits[...] - peak) / total).astype(BF16)
    combine[...] = weights
    part = dot(weights[:, :count], cotangent[...], 1, 0)
    part += dot(weights[:, count:], cotangent_other[...], 1, 0)
    out[:, :, :width] = sums[...]
    out[:, :, width : 2 * width] = part.astype(BF16).reshape(sums.shape)
    out[:, :, 2 * width :] = stats[...]


def merge(message):
    width = (message.shape[2] - TAIL) // 2
    stats = message[:, :, 2 * width : 2 * width + 128]
    peaks, totals = read_stat(stats, 0), read_stat(stats, 1)
    top = jnp.max(peaks, axis=0, keepdims=True)
    scales = jnp.exp(peaks - top)
    total = jnp.sum(totals * scales, axis=0)
    first = message[0, :, :width].astype(F32) * scales[0]
    for p in range(1, message.shape[0]):
        first += message[p, :, :width].astype(F32) * scales[p]
    second = message[0, :, width : 2 * width].astype(F32)
    for p in range(1, message.shape[0]):
        second += message[p, :, width : 2 * width].astype(F32)
    return first, second, top[0], total


def merge_kernel(message, out):
    width = (message.shape[2] - TAIL) // 2
    first, second, top, total = merge(message)
    first, second = first.astype(BF16), second.astype(BF16)
    block = stat_block([top, total]).astype(BF16)
    for i in range(out.shape[0]):
        out[i, :, :width] = first
        out[i, :, width : 2 * width] = second
        out[i, :, 2 * width :] = block


def expert_kernel(
    message, w_in, w_out, parts, sums, stats, slot_in_out, out_grad_out, hidden_out, pre_grad_out
):
    width = sums.shape[1]
    first, second, top, total = merge(message)
    slot_sum = first / total
    sums[...] = slot_sum
    lane = lax.broadcasted_iota(jnp.int32, stats.shape, 1)
    stats[...] = jnp.where(lane == 0, top, total)
    slot_in = slot_sum.astype(BF16)
    out_grad = second.astype(BF16)
    slot_in_out[...] = slot_in
    out_grad_out[...] = out_grad
    pre_act = dot(slot_in, w_in[...], 1, 0)
    tanh = jnp.tanh(ROOT * (pre_act + CUBE * (pre_act * pre_act * pre_act)))
    hidden = (pre_act * (0.5 * (1.0 + tanh))).astype(BF16)
    hidden_out[...] = hidden
    act_grad = dot(out_grad, w_out[...], 1, 1)
    slope = 0.5 * (1.0 + tanh) + 0.5 * pre_act * (1.0 - tanh * tanh) * (
        ROOT * (1.0 + 3.0 * CUBE * (pre_act * pre_act))
    )
    pre_grad = (act_grad * slope).astype(BF16)
    pre_grad_out[...] = pre_grad
    out_part = dot(hidden, w_out[...], 1, 0).astype(BF16)
    slot_part = dot(pre_grad, w_in[...], 1, 1).astype(BF16)
    for i in range(parts.shape[0]):
        parts[i, :, :width] = out_part
        parts[i, :, width:] = slot_part


def outs_kernel(parts, sums, stats, out):
    width = sums.shape[1]
    total = parts[0].astype(F32)
    for p in range(1, parts.shape[0]):
        total += parts[p].astype(F32)
    values = total.astype(BF16)
    crossing = jnp.sum(values[:, width:].astype(F32) * sums[...], axis=1, keepdims=True)
    block = stat_block([stats[:, 0:1], stats[:, 1:2], crossing]).astype(BF16)
    for i in range(out.shape[0]):
        out[i, :, : 2 * width] = values
        out[i, :, 2 * width :] = block


def combine_dot_kernel(outs, cotangent, cotangent_other, combine, dots, columns):
    width = cotangent.shape[1]
    slot_out = outs[:, :, :width].reshape(combine.shape[0], width)
    value = jnp.concatenate(
        [dot(slot_out, cotangent[...], 1, 1), dot(slot_out, cotangent_other[...], 1, 1)], axis=1
    )
    dots[...] = value
    part = jnp.sum(combine[...].astype(F32) * value, axis=0, keepdims=True)
    columns[...] = jnp.concatenate([part, part], axis=0)


def pick_kernel(outs, tokens, tokens_other, logits, dispatch, term):
    own, width = logits.shape[0], tokens.shape[1]
    block = outs[:, :, 2 * width : 2 * width + 128].reshape(own, 128).astype(F32)
    peak, total, crossing = (read_stat(block, i) for i in range(3))
    weights = (jnp.exp(logits[...] - peak) / total).astype(BF16)
    dispatch[...] = weights
    slot_grad = outs[:, :, width : 2 * width].reshape(own, width)
    value = jnp.concatenate(
        [dot(slot_grad, tokens[...], 1, 1), dot(slot_grad, tokens_other[...], 1, 1)], axis=1
    )
    term[...] = weights.astype(F32) * (value - crossing)


def key_kernel(
    outs, term, dots, combine, columns, columns_other, dispatch, keys, tokens, tokens_other,
    out, pack, weights,
):
    count, width = tokens.shape
    own = keys.shape[0]
    column = columns[0:1, :] + turn(columns_other[...], count)[0:1]
    combine_grad = combine[...].astype(F32) * (dots[...] - column)
    logit_grad = (term[...] + combine_grad).astype(BF16)
    part = dot(logit_grad[:, :count], tokens[...], 1, 0)
    part += dot(logit_grad[:, count:], tokens_other[...], 1, 0)
    out[...] = part.astype(BF16).reshape(out.shape)
    pack[:, :width] = outs[:, :, :width].reshape(own, width)
    pack[:, width : 2 * width] = outs[:, :, width : 2 * width].reshape(own, width)
    pack[:, 2 * width : 3 * width] = keys[...]
    for i, values in enumerate((combine[...], dispatch[...], logit_grad)):
        pack[:, 3 * width + i * count : 3 * width + (i + 1) * count] = values[:, count:]
        weights[:, i * count : (i + 1) * count] = values[:, :count]


def token_kernel(pack, pack_other, weights, slot_out, rest, combine, rest_weights):
    own = pack.shape[0]
    width = slot_out.shape[1]
    count = combine.shape[1]
    other = pack_other[:, 3 * width :]
    slot_out[:own] = pack[:, :width]
    slot_out[own:] = pack_other[:, :width]
    combine[:own] = weights[:, :count]
    combine[own:] = other[:, :count]
    for i in range(2):
        cols = slice((i + 1) * width, (i + 2) * width)
        rest[2 * i * own : (2 * i + 1) * own] = pack[:, cols]
        rest[(2 * i + 1) * own : (2 * i + 2) * own] = pack_other[:, cols]
        cols = slice((i + 1) * count, (i + 2) * count)
        rest_weights[2 * i * own : (2 * i + 1) * own] = weights[:, cols]
        rest_weights[(2 * i + 1) * own : (2 * i + 2) * own] = other[:, cols]


def key_merge_kernel(message, out):
    total = message[0].astype(F32)
    for p in range(1, message.shape[0]):
        total += message[p].astype(F32)
    for i in range(out.shape[0]):
        out[i] = total.astype(out.dtype)


def key_sum_kernel(message, out):
    total = message[0].astype(F32)
    for p in range(1, message.shape[0]):
        total += message[p].astype(F32)
    out[...] = total


def call(kernel, outs, *args, vmem=True):
    whole = pl.BlockSpec(memory_space=pltpu.VMEM)
    make = pltpu.VMEM if vmem else jax.ShapeDtypeStruct
    return pl.pallas_call(
        kernel,
        out_shape=[make(shape, dtype) for shape, dtype in outs],
        in_specs=[whole] * len(args),
        out_specs=[whole] * len(outs),
        compiler_params=pltpu.CompilerParams(vmem_limit_bytes=24 * 1024 * 1024),
    )(*args)


def body(tokens, slot_keys, w_in, w_out, cotangent):
    count, width = tokens.shape
    hidden_units = w_in.shape[2]
    seq = lax.axis_size("seq")
    experts = lax.axis_size("expert")
    rows = slot_keys.shape[0]
    half = experts // 2
    own = half * rows
    both = 2 * count
    long = 2 * width + TAIL
    order = [4 * i + 2 * j for j in range(2) for i in range(half // 2)]
    same_core = [[i + c for i in order] for c in range(2)]
    partner = [(i, i ^ 1) for i in range(experts)]

    def swap(values):
        return lax.ppermute(values, "expert", partner)

    def exchange(values):
        return lax.all_to_all(values, "expert", 0, 0, tiled=True, axis_index_groups=same_core)

    def exchange_seq(values):
        return lax.all_to_all(values, "seq", 0, 0, tiled=True)

    tokens_other, cotangent_other = swap(tokens), swap(cotangent)
    (message,) = call(copies_kernel, [((half, rows, width), BF16)], slot_keys)
    keys, logits, columns = call(
        logit_kernel,
        [((own, width), BF16), ((own, both), F32), ((2, both), F32)],
        exchange(message), tokens, tokens_other,
    )
    columns_other = swap(columns)
    sums, stats = call(
        dispatch_kernel,
        [((half, rows, width), BF16), ((half, rows, TAIL), BF16)],
        logits, tokens, tokens_other,
    )
    combine, message = call(
        combine_kernel,
        [((own, both), BF16), ((half, rows, long), BF16)],
        logits, columns, columns_other, cotangent, cotangent_other, sums, stats,
    )
    (message,) = call(merge_kernel, [((seq, rows, long), BF16)], exchange(message))
    parts, sums, stats, slot_in, out_grad, hidden, pre_grad = call(
        expert_kernel,
        [
            ((seq, rows, 2 * width), BF16),
            ((rows, width), F32),
            ((rows, 128), F32),
            ((rows, width), BF16),
            ((rows, width), BF16),
            ((rows, hidden_units), BF16),
            ((rows, hidden_units), BF16),
        ],
        exchange_seq(message), w_in[0], w_out[0],
    )
    (message,) = call(
        outs_kernel, [((half, rows, long), BF16)], exchange_seq(parts), sums, stats
    )
    outs = exchange(message)
    dots, columns = call(
        combine_dot_kernel,
        [((own, both), F32), ((2, both), F32)],
        outs, cotangent, cotangent_other, combine,
    )
    columns_other = swap(columns)
    dispatch, term = call(
        pick_kernel,
        [((own, both), BF16), ((own, both), F32)],
        outs, tokens, tokens_other, logits,
    )
    message, pack, weights = call(
        key_kernel,
        [
            ((half, rows, width), BF16),
            ((own, 3 * width + 3 * count), BF16),
            ((own, 3 * count), BF16),
        ],
        outs, term, dots, combine, columns, columns_other, dispatch, keys, tokens, tokens_other,
    )
    (message,) = call(key_merge_kernel, [((seq, rows, width), BF16)], exchange(message))
    (key_grad,) = call(key_sum_kernel, [((rows, width), F32)], exchange_seq(message), vmem=False)

    slot_out, rest, combine, rest_weights = call(
        token_kernel,
        [
            ((2 * own, width), BF16),
            ((4 * own, width), BF16),
            ((2 * own, count), BF16),
            ((4 * own, count), BF16),
        ],
        pack, swap(pack), weights,
    )
    w_out_grad = dot(hidden, out_grad, 0, 0).astype(BF16)[None]
    w_in_grad = dot(slot_in, pre_grad, 0, 0).astype(BF16)[None]
    layer_out = dot(combine, slot_out, 0, 0).astype(BF16)
    token_grad = dot(rest_weights, rest, 0, 0).astype(BF16)
    return (layer_out, token_grad, key_grad, w_in_grad, w_out_grad)


def solution(mesh):
    in_specs = (
        P(("seq", "expert"), None),
        P("expert", None),
        P("expert", None, "seq"),
        P("expert", "seq", None),
        P(("seq", "expert"), None),
    )
    out_specs = (
        P(("seq", "expert"), None),
        P(("seq", "expert"), None),
        P("expert", None),
        P("expert", None, "seq"),
        P("expert", "seq", None),
    )
    return jax.shard_map(body, mesh=mesh, in_specs=in_specs, out_specs=out_specs, check_vma=False)
```

```python
import math

import jax
import jax.numpy as jnp
from jax import lax
from jax.experimental import pallas as pl
from jax.experimental.pallas import tpu as pltpu
from jax.sharding import PartitionSpec as P

F32 = jnp.float32
BF16 = jnp.bfloat16
TAIL = 256
ROOT = math.sqrt(2.0 / math.pi)
CUBE = 0.044715


def dot(a, b, a_dim, b_dim):
    return lax.dot_general(a, b, (((a_dim,), (b_dim,)), ((), ())), preferred_element_type=F32)


def pieces(values):
    high = values.astype(BF16).astype(F32)
    rest = values - high
    middle = rest.astype(BF16).astype(F32)
    return [high, middle, rest - middle]


def stat_block(stats):
    lane = lax.broadcasted_iota(jnp.int32, (stats[0].shape[0], TAIL), 1)
    block = jnp.zeros(lane.shape, F32)
    for i, piece in enumerate([p for s in stats for p in pieces(s)]):
        block = jnp.where(lane == i, piece, block)
    return block


def read_stat(block, i):
    cols = [block[..., k : k + 1].astype(F32) for k in range(3 * i, 3 * i + 3)]
    return cols[0] + cols[1] + cols[2]


def bit_reversed(size):
    bits = size.bit_length() - 1
    return sorted(range(size), key=lambda i: [i >> k & 1 for k in range(bits)])


def copies_kernel(values, out):
    for i in range(out.shape[0]):
        out[i] = values[...]


def logit_kernel(message, tokens, tokens_other, keys, logits, columns):
    own, width = keys.shape
    keys[...] = message[...].reshape(own, width)
    value = jnp.concatenate(
        [dot(keys[...], tokens[...], 1, 1), dot(keys[...], tokens_other[...], 1, 1)], axis=1
    )
    logits[...] = value
    peak = jnp.max(value, axis=0, keepdims=True)
    columns[0:1, :] = peak
    columns[1:2, :] = jnp.sum(jnp.exp(value - peak), axis=0, keepdims=True)


def dispatch_kernel(logits, tokens, tokens_other, sums, stats):
    count = tokens.shape[0]
    value = logits[...]
    peak = jnp.max(value, axis=1, keepdims=True)
    weights = jnp.exp(value - peak)
    total = jnp.sum(weights, axis=1, keepdims=True)
    weights = weights.astype(BF16)
    part = dot(weights[:, :count], tokens[...], 1, 0)
    part += dot(weights[:, count:], tokens_other[...], 1, 0)
    sums[...] = part.astype(BF16).reshape(sums.shape)
    stats[...] = stat_block([peak, total]).astype(BF16).reshape(stats.shape)


def turn(columns, count):
    return jnp.concatenate([columns[:, count:], columns[:, :count]], axis=1)


def combine_kernel(logits, columns, columns_other, cotangent, cotangent_other, sums, stats, combine, out):
    count, width = cotangent.shape
    other = turn(columns_other[...], count)
    here = columns[...]
    peak = jnp.maximum(here[0:1], other[0:1])
    total = here[1:2] * jnp.exp(here[0:1] - peak) + other[1:2] * jnp.exp(other[0:1] - peak)
    weights = (jnp.exp(logits[...] - peak) / total).astype(BF16)
    combine[...] = weights
    part = dot(weights[:, :count], cotangent[...], 1, 0)
    part += dot(weights[:, count:], cotangent_other[...], 1, 0)
    out[:, :, :width] = sums[...]
    out[:, :, width : 2 * width] = part.astype(BF16).reshape(sums.shape)
    out[:, :, 2 * width :] = stats[...]


def merge(message):
    width = (message.shape[2] - TAIL) // 2
    stats = message[:, :, 2 * width : 2 * width + 128]
    peaks, totals = read_stat(stats, 0), read_stat(stats, 1)
    top = jnp.max(peaks, axis=0, keepdims=True)
    scales = jnp.exp(peaks - top)
    total = jnp.sum(totals * scales, axis=0)
    first = message[0, :, :width].astype(F32) * scales[0]
    for p in range(1, message.shape[0]):
        first += message[p, :, :width].astype(F32) * scales[p]
    second = message[0, :, width : 2 * width].astype(F32)
    for p in range(1, message.shape[0]):
        second += message[p, :, width : 2 * width].astype(F32)
    return first, second, top[0], total


def merge_kernel(message, out):
    width = (message.shape[2] - TAIL) // 2
    first, second, top, total = merge(message)
    first, second = first.astype(BF16), second.astype(BF16)
    block = stat_block([top, total]).astype(BF16)
    for i in range(out.shape[0]):
        out[i, :, :width] = first
        out[i, :, width : 2 * width] = second
        out[i, :, 2 * width :] = block


def expert_kernel(
    message, w_in, w_out, parts, sums, stats, slot_in_out, out_grad_out, hidden_out, pre_grad_out
):
    width = sums.shape[1]
    first, second, top, total = merge(message)
    slot_sum = first / total
    sums[...] = slot_sum
    lane = lax.broadcasted_iota(jnp.int32, stats.shape, 1)
    stats[...] = jnp.where(lane == 0, top, total)
    slot_in = slot_sum.astype(BF16)
    out_grad = second.astype(BF16)
    slot_in_out[...] = slot_in
    out_grad_out[...] = out_grad
    pre_act = dot(slot_in, w_in[...], 1, 0)
    tanh = jnp.tanh(ROOT * (pre_act + CUBE * (pre_act * pre_act * pre_act)))
    hidden = (pre_act * (0.5 * (1.0 + tanh))).astype(BF16)
    hidden_out[...] = hidden
    act_grad = dot(out_grad, w_out[...], 1, 1)
    slope = 0.5 * (1.0 + tanh) + 0.5 * pre_act * (1.0 - tanh * tanh) * (
        ROOT * (1.0 + 3.0 * CUBE * (pre_act * pre_act))
    )
    pre_grad = (act_grad * slope).astype(BF16)
    pre_grad_out[...] = pre_grad
    out_part = dot(hidden, w_out[...], 1, 0).astype(BF16)
    slot_part = dot(pre_grad, w_in[...], 1, 1).astype(BF16)
    for i in range(parts.shape[0]):
        parts[i, :, :width] = out_part
        parts[i, :, width:] = slot_part


def outs_kernel(parts, sums, stats, out):
    width = sums.shape[1]
    total = parts[0].astype(F32)
    for p in range(1, parts.shape[0]):
        total += parts[p].astype(F32)
    values = total.astype(BF16)
    crossing = jnp.sum(values[:, width:].astype(F32) * sums[...], axis=1, keepdims=True)
    block = stat_block([stats[:, 0:1], stats[:, 1:2], crossing]).astype(BF16)
    for i in range(out.shape[0]):
        out[i, :, : 2 * width] = values
        out[i, :, 2 * width :] = block


def combine_dot_kernel(outs, cotangent, cotangent_other, combine, dots, columns):
    width = cotangent.shape[1]
    slot_out = outs[:, :, :width].reshape(combine.shape[0], width)
    value = jnp.concatenate(
        [dot(slot_out, cotangent[...], 1, 1), dot(slot_out, cotangent_other[...], 1, 1)], axis=1
    )
    dots[...] = value
    part = jnp.sum(combine[...].astype(F32) * value, axis=0, keepdims=True)
    columns[...] = jnp.concatenate([part, part], axis=0)


def pick_kernel(outs, tokens, tokens_other, logits, dispatch, term):
    own, width = logits.shape[0], tokens.shape[1]
    block = outs[:, :, 2 * width : 2 * width + 128].reshape(own, 128).astype(F32)
    peak, total, crossing = (read_stat(block, i) for i in range(3))
    weights = (jnp.exp(logits[...] - peak) / total).astype(BF16)
    dispatch[...] = weights
    slot_grad = outs[:, :, width : 2 * width].reshape(own, width)
    value = jnp.concatenate(
        [dot(slot_grad, tokens[...], 1, 1), dot(slot_grad, tokens_other[...], 1, 1)], axis=1
    )
    term[...] = weights.astype(F32) * (value - crossing)


def key_kernel(
    term, dots, combine, columns, columns_other, tokens, tokens_other, out, logit_grad_out
):
    count = tokens.shape[0]
    column = columns[0:1, :] + turn(columns_other[...], count)[0:1]
    combine_grad = combine[...].astype(F32) * (dots[...] - column)
    logit_grad = (term[...] + combine_grad).astype(BF16)
    part = dot(logit_grad[:, :count], tokens[...], 1, 0)
    part += dot(logit_grad[:, count:], tokens_other[...], 1, 0)
    out[...] = part.astype(BF16).reshape(out.shape)
    logit_grad_out[...] = logit_grad


def pack_kernel(outs, keys, combine, dispatch, logit_grad, pack, weights):
    own, width = keys.shape
    count = weights.shape[1] // 3
    pack[:, :width] = outs[:, :, :width].reshape(own, width)
    pack[:, width : 2 * width] = outs[:, :, width : 2 * width].reshape(own, width)
    pack[:, 2 * width : 3 * width] = keys[...]
    for i, values in enumerate((combine[...], dispatch[...], logit_grad[...])):
        pack[:, 3 * width + i * count : 3 * width + (i + 1) * count] = values[:, count:]
        weights[:, i * count : (i + 1) * count] = values[:, :count]


def token_kernel(pack, pack_other, weights, *refs):
    slot_out, rest, combine, rest_weights = refs[4:8]
    for here, there in zip(refs[:4], refs[8:]):
        there[...] = here[...]
    own = pack.shape[0]
    width = slot_out.shape[1]
    count = combine.shape[1]
    other = pack_other[:, 3 * width :]
    slot_out[:own] = pack[:, :width]
    slot_out[own:] = pack_other[:, :width]
    combine[:own] = weights[:, :count]
    combine[own:] = other[:, :count]
    for i in range(2):
        cols = slice((i + 1) * width, (i + 2) * width)
        rest[2 * i * own : (2 * i + 1) * own] = pack[:, cols]
        rest[(2 * i + 1) * own : (2 * i + 2) * own] = pack_other[:, cols]
        cols = slice((i + 1) * count, (i + 2) * count)
        rest_weights[2 * i * own : (2 * i + 1) * own] = weights[:, cols]
        rest_weights[(2 * i + 1) * own : (2 * i + 2) * own] = other[:, cols]


def key_merge_kernel(message, *refs):
    out = refs[-1]
    total = message[0].astype(F32)
    for p in range(1, message.shape[0]):
        total += message[p].astype(F32)
    for i in range(out.shape[0]):
        out[i] = total.astype(out.dtype)


def key_sum_kernel(message, out):
    total = message[0].astype(F32)
    for p in range(1, message.shape[0]):
        total += message[p].astype(F32)
    out[...] = total


def call(kernel, outs, *args, vmem=True, far=()):
    whole = pl.BlockSpec(memory_space=pltpu.VMEM)
    there = pl.BlockSpec(memory_space=pltpu.HBM)
    make = pltpu.VMEM if vmem else jax.ShapeDtypeStruct
    args = [
        pltpu.with_memory_space_constraint(a, pltpu.HBM) if i in far else a
        for i, a in enumerate(args)
    ]
    return pl.pallas_call(
        kernel,
        out_shape=[make(shape, dtype) for shape, dtype in outs],
        in_specs=[there if i in far else whole for i in range(len(args))],
        out_specs=[whole] * len(outs),
        compiler_params=pltpu.CompilerParams(vmem_limit_bytes=24 * 1024 * 1024),
    )(*args)


def body(tokens, slot_keys, w_in, w_out, cotangent):
    count, width = tokens.shape
    hidden_units = w_in.shape[2]
    seq = lax.axis_size("seq")
    experts = lax.axis_size("expert")
    rows = slot_keys.shape[0]
    half = experts // 2
    own = half * rows
    both = 2 * count
    long = 2 * width + TAIL
    order = [4 * i + 2 * j for j in range(2) for i in bit_reversed(half // 2)]
    same_core = [[i + c for i in order] for c in range(2)]
    partner = [(i, i ^ 1) for i in range(experts)]

    def swap(values):
        return lax.ppermute(values, "expert", partner)

    def exchange(values):
        return lax.all_to_all(values, "expert", 0, 0, tiled=True, axis_index_groups=same_core)

    def exchange_seq(values):
        return lax.all_to_all(values, "seq", 0, 0, tiled=True)

    tokens_other, cotangent_other = swap(tokens), swap(cotangent)
    (message,) = call(copies_kernel, [((half, rows, width), BF16)], slot_keys)
    keys, logits, columns = call(
        logit_kernel,
        [((own, width), BF16), ((own, both), F32), ((2, both), F32)],
        exchange(message), tokens, tokens_other,
    )
    columns_other = swap(columns)
    sums, stats = call(
        dispatch_kernel,
        [((half, rows, width), BF16), ((half, rows, TAIL), BF16)],
        logits, tokens, tokens_other,
    )
    combine, message = call(
        combine_kernel,
        [((own, both), BF16), ((half, rows, long), BF16)],
        logits, columns, columns_other, cotangent, cotangent_other, sums, stats,
    )
    (message,) = call(merge_kernel, [((seq, rows, long), BF16)], exchange(message))
    parts, sums, stats, slot_in, out_grad, hidden, pre_grad = call(
        expert_kernel,
        [
            ((seq, rows, 2 * width), BF16),
            ((rows, width), F32),
            ((rows, 128), F32),
            ((rows, width), BF16),
            ((rows, width), BF16),
            ((rows, hidden_units), BF16),
            ((rows, hidden_units), BF16),
        ],
        exchange_seq(message), w_in[0], w_out[0],
    )
    (message,) = call(
        outs_kernel, [((half, rows, long), BF16)], exchange_seq(parts), sums, stats
    )
    outs = exchange(message)
    dots, columns = call(
        combine_dot_kernel,
        [((own, both), F32), ((2, both), F32)],
        outs, cotangent, cotangent_other, combine,
    )
    columns_other = swap(columns)
    dispatch, term = call(
        pick_kernel,
        [((own, both), BF16), ((own, both), F32)],
        outs, tokens, tokens_other, logits,
    )
    message, logit_grad = call(
        key_kernel,
        [((half, rows, width), BF16), ((own, both), BF16)],
        term, dots, combine, columns, columns_other, tokens, tokens_other,
    )
    message = exchange(message)
    pack, weights = call(
        pack_kernel,
        [((own, 3 * width + 3 * count), BF16), ((own, 3 * count), BF16)],
        outs, keys, combine, dispatch, logit_grad,
    )
    factors = (slot_in, out_grad, hidden, pre_grad)
    slot_out, rest, combine, rest_weights, slot_in, out_grad, hidden, pre_grad = call(
        token_kernel,
        [
            ((2 * own, width), BF16),
            ((4 * own, width), BF16),
            ((2 * own, count), BF16),
            ((4 * own, count), BF16),
        ]
        + [(v.shape, v.dtype) for v in factors],
        pack, swap(pack), weights, *factors,
    )
    layer_out = dot(combine, slot_out, 0, 0).astype(BF16)
    token_grad = dot(rest_weights, rest, 0, 0).astype(BF16)
    w_out_grad = dot(hidden, out_grad, 0, 0).astype(BF16)[None]
    w_in_grad = dot(slot_in, pre_grad, 0, 0).astype(BF16)[None]
    results = (layer_out, token_grad, w_in_grad, w_out_grad)
    (message,) = call(
        key_merge_kernel, [((seq, rows, width), BF16)], message, *results, far=(1, 2, 3, 4)
    )
    (key_grad,) = call(key_sum_kernel, [((rows, width), F32)], exchange_seq(message), vmem=False)

    return (layer_out, token_grad, key_grad, w_in_grad, w_out_grad)


def solution(mesh):
    in_specs = (
        P(("seq", "expert"), None),
        P("expert", None),
        P("expert", None, "seq"),
        P("expert", "seq", None),
        P(("seq", "expert"), None),
    )
    out_specs = (
        P(("seq", "expert"), None),
        P(("seq", "expert"), None),
        P("expert", None),
        P("expert", None, "seq"),
        P("expert", "seq", None),
    )
    return jax.shard_map(body, mesh=mesh, in_specs=in_specs, out_specs=out_specs, check_vma=False)
```

```python
import math

import jax
import jax.numpy as jnp
from jax import lax
from jax.experimental import pallas as pl
from jax.experimental.pallas import tpu as pltpu
from jax.sharding import PartitionSpec as P

F32 = jnp.float32
BF16 = jnp.bfloat16
TAIL = 256
ROOT = math.sqrt(2.0 / math.pi)
CUBE = 0.044715


def dot(a, b, a_dim, b_dim):
    return lax.dot_general(a, b, (((a_dim,), (b_dim,)), ((), ())), preferred_element_type=F32)


def pieces(values):
    high = values.astype(BF16).astype(F32)
    rest = values - high
    middle = rest.astype(BF16).astype(F32)
    return [high, middle, rest - middle]


def stat_block(stats):
    lane = lax.broadcasted_iota(jnp.int32, (stats[0].shape[0], TAIL), 1)
    block = jnp.zeros(lane.shape, F32)
    for i, piece in enumerate([p for s in stats for p in pieces(s)]):
        block = jnp.where(lane == i, piece, block)
    return block


def read_stat(block, i):
    cols = [block[..., k : k + 1].astype(F32) for k in range(3 * i, 3 * i + 3)]
    return cols[0] + cols[1] + cols[2]


def copies_kernel(values, out):
    for i in range(out.shape[0]):
        out[i] = values[...]


def logit_kernel(message, tokens, tokens_other, keys, logits, columns, tokens_both):
    own, width = keys.shape
    count = tokens.shape[0]
    keys[...] = message[...].reshape(own, width)
    tokens_both[:count] = tokens[...]
    tokens_both[count:] = tokens_other[...]
    value = dot(keys[...], tokens_both[...], 1, 1)
    logits[...] = value
    peak = jnp.max(value, axis=0, keepdims=True)
    columns[0:1, :] = peak
    columns[1:2, :] = jnp.sum(jnp.exp(value - peak), axis=0, keepdims=True)


def dispatch_kernel(logits, tokens_both, cotangent, cotangent_other, sums, stats, cotangent_both):
    count = cotangent.shape[0]
    cotangent_both[:count] = cotangent[...]
    cotangent_both[count:] = cotangent_other[...]
    value = logits[...]
    peak = jnp.max(value, axis=1, keepdims=True)
    weights = jnp.exp(value - peak)
    total = jnp.sum(weights, axis=1, keepdims=True)
    part = dot(weights.astype(BF16), tokens_both[...], 1, 0)
    sums[...] = part.astype(BF16).reshape(sums.shape)
    stats[...] = stat_block([peak, total]).astype(BF16).reshape(stats.shape)


def turn(columns, count):
    return jnp.concatenate([columns[:, count:], columns[:, :count]], axis=1)


def combine_kernel(logits, columns, columns_other, cotangent_both, sums, stats, combine, out):
    count, width = cotangent_both.shape[0] // 2, cotangent_both.shape[1]
    other = turn(columns_other[...], count)
    here = columns[...]
    peak = jnp.maximum(here[0:1], other[0:1])
    total = here[1:2] * jnp.exp(here[0:1] - peak) + other[1:2] * jnp.exp(other[0:1] - peak)
    weights = (jnp.exp(logits[...] - peak) / total).astype(BF16)
    combine[...] = weights
    part = dot(weights, cotangent_both[...], 1, 0)
    out[:, :, :width] = sums[...]
    out[:, :, width : 2 * width] = part.astype(BF16).reshape(sums.shape)
    out[:, :, 2 * width :] = stats[...]


def merge(message):
    width = (message.shape[2] - TAIL) // 2
    stats = message[:, :, 2 * width : 2 * width + 128]
    peaks, totals = read_stat(stats, 0), read_stat(stats, 1)
    top = jnp.max(peaks, axis=0, keepdims=True)
    scales = jnp.exp(peaks - top)
    total = jnp.sum(totals * scales, axis=0)
    first = message[0, :, :width].astype(F32) * scales[0]
    for p in range(1, message.shape[0]):
        first += message[p, :, :width].astype(F32) * scales[p]
    second = message[0, :, width : 2 * width].astype(F32)
    for p in range(1, message.shape[0]):
        second += message[p, :, width : 2 * width].astype(F32)
    return first, second, top[0], total


def merge_kernel(message, out):
    width = (message.shape[2] - TAIL) // 2
    first, second, top, total = merge(message)
    first, second = first.astype(BF16), second.astype(BF16)
    block = stat_block([top, total]).astype(BF16)
    for i in range(out.shape[0]):
        out[i, :, :width] = first
        out[i, :, width : 2 * width] = second
        out[i, :, 2 * width :] = block


def expert_kernel(
    message, w_in, w_out, parts, sums, stats, slot_in_out, out_grad_out, hidden_out, pre_grad_out
):
    width = sums.shape[1]
    first, second, top, total = merge(message)
    slot_sum = first / total
    sums[...] = slot_sum
    lane = lax.broadcasted_iota(jnp.int32, stats.shape, 1)
    stats[...] = jnp.where(lane == 0, top, total)
    slot_in = slot_sum.astype(BF16)
    out_grad = second.astype(BF16)
    slot_in_out[...] = slot_in
    out_grad_out[...] = out_grad
    pre_act = dot(slot_in, w_in[...], 1, 0)
    tanh = jnp.tanh(ROOT * (pre_act + CUBE * (pre_act * pre_act * pre_act)))
    hidden = (pre_act * (0.5 * (1.0 + tanh))).astype(BF16)
    hidden_out[...] = hidden
    act_grad = dot(out_grad, w_out[...], 1, 1)
    slope = 0.5 * (1.0 + tanh) + 0.5 * pre_act * (1.0 - tanh * tanh) * (
        ROOT * (1.0 + 3.0 * CUBE * (pre_act * pre_act))
    )
    pre_grad = (act_grad * slope).astype(BF16)
    pre_grad_out[...] = pre_grad
    out_part = dot(hidden, w_out[...], 1, 0).astype(BF16)
    slot_part = dot(pre_grad, w_in[...], 1, 1).astype(BF16)
    for i in range(parts.shape[0]):
        parts[i, :, :width] = out_part
        parts[i, :, width:] = slot_part


def outs_kernel(parts, sums, stats, out):
    width = sums.shape[1]
    total = parts[0].astype(F32)
    for p in range(1, parts.shape[0]):
        total += parts[p].astype(F32)
    values = total.astype(BF16)
    crossing = jnp.sum(values[:, width:].astype(F32) * sums[...], axis=1, keepdims=True)
    block = stat_block([stats[:, 0:1], stats[:, 1:2], crossing]).astype(BF16)
    for i in range(out.shape[0]):
        out[i, :, : 2 * width] = values
        out[i, :, 2 * width :] = block


def combine_dot_kernel(outs, cotangent_both, combine, dots, columns):
    width = cotangent_both.shape[1]
    slot_out = outs[:, :, :width].reshape(combine.shape[0], width)
    value = dot(slot_out, cotangent_both[...], 1, 1)
    dots[...] = value
    part = jnp.sum(combine[...].astype(F32) * value, axis=0, keepdims=True)
    columns[...] = jnp.concatenate([part, part], axis=0)


def pick_kernel(outs, tokens_both, logits, dispatch, term):
    own, width = logits.shape[0], tokens_both.shape[1]
    block = outs[:, :, 2 * width : 2 * width + 128].reshape(own, 128).astype(F32)
    peak, total, crossing = (read_stat(block, i) for i in range(3))
    weights = (jnp.exp(logits[...] - peak) / total).astype(BF16)
    dispatch[...] = weights
    slot_grad = outs[:, :, width : 2 * width].reshape(own, width)
    value = dot(slot_grad, tokens_both[...], 1, 1)
    term[...] = weights.astype(F32) * (value - crossing)


def key_kernel(
    term, dots, combine, columns, columns_other, tokens_both, out, logit_grad_out
):
    count = tokens_both.shape[0] // 2
    column = columns[0:1, :] + turn(columns_other[...], count)[0:1]
    combine_grad = combine[...].astype(F32) * (dots[...] - column)
    logit_grad = (term[...] + combine_grad).astype(BF16)
    part = dot(logit_grad, tokens_both[...], 1, 0)
    out[...] = part.astype(BF16).reshape(out.shape)
    logit_grad_out[...] = logit_grad


def pack_kernel(outs, keys, combine, dispatch, logit_grad, pack, weights):
    own, width = keys.shape
    count = weights.shape[1] // 3
    pack[:, :width] = outs[:, :, :width].reshape(own, width)
    pack[:, width : 2 * width] = outs[:, :, width : 2 * width].reshape(own, width)
    pack[:, 2 * width : 3 * width] = keys[...]
    for i, values in enumerate((combine[...], dispatch[...], logit_grad[...])):
        pack[:, 3 * width + i * count : 3 * width + (i + 1) * count] = values[:, count:]
        weights[:, i * count : (i + 1) * count] = values[:, :count]


def token_kernel(pack, pack_other, weights, *refs):
    slot_out, rest, combine, rest_weights = refs[4:8]
    for here, there in zip(refs[:4], refs[8:]):
        there[...] = here[...]
    own = pack.shape[0]
    width = slot_out.shape[1]
    count = combine.shape[1]
    other = pack_other[:, 3 * width :]
    slot_out[:own] = pack[:, :width]
    slot_out[own:] = pack_other[:, :width]
    combine[:own] = weights[:, :count]
    combine[own:] = other[:, :count]
    for i in range(2):
        cols = slice((i + 1) * width, (i + 2) * width)
        rest[2 * i * own : (2 * i + 1) * own] = pack[:, cols]
        rest[(2 * i + 1) * own : (2 * i + 2) * own] = pack_other[:, cols]
        cols = slice((i + 1) * count, (i + 2) * count)
        rest_weights[2 * i * own : (2 * i + 1) * own] = weights[:, cols]
        rest_weights[(2 * i + 1) * own : (2 * i + 2) * own] = other[:, cols]


def key_merge_kernel(message, *refs):
    out = refs[-1]
    total = message[0].astype(F32)
    for p in range(1, message.shape[0]):
        total += message[p].astype(F32)
    for i in range(out.shape[0]):
        out[i] = total.astype(out.dtype)


def key_sum_kernel(message, out):
    total = message[0].astype(F32)
    for p in range(1, message.shape[0]):
        total += message[p].astype(F32)
    out[...] = total


def call(kernel, outs, *args, vmem=True, far=()):
    whole = pl.BlockSpec(memory_space=pltpu.VMEM)
    there = pl.BlockSpec(memory_space=pltpu.HBM)
    make = pltpu.VMEM if vmem else jax.ShapeDtypeStruct
    args = [
        pltpu.with_memory_space_constraint(a, pltpu.HBM) if i in far else a
        for i, a in enumerate(args)
    ]
    return pl.pallas_call(
        kernel,
        out_shape=[make(shape, dtype) for shape, dtype in outs],
        in_specs=[there if i in far else whole for i in range(len(args))],
        out_specs=[whole] * len(outs),
        compiler_params=pltpu.CompilerParams(vmem_limit_bytes=24 * 1024 * 1024),
    )(*args)


def body(tokens, slot_keys, w_in, w_out, cotangent):
    count, width = tokens.shape
    hidden_units = w_in.shape[2]
    seq = lax.axis_size("seq")
    experts = lax.axis_size("expert")
    rows = slot_keys.shape[0]
    half = experts // 2
    own = half * rows
    both = 2 * count
    long = 2 * width + TAIL
    order = [4 * i + 2 * j for j in (1, 0) for i in (4, 6, 5, 7, 2, 3, 1, 0)]
    seq_order = [6, 7, 2, 3, 5, 1, 4, 0]
    same_core = [[i + c for i in order] for c in range(2)]
    partner = [(i, i ^ 1) for i in range(experts)]

    def swap(values):
        return lax.ppermute(values, "expert", partner)

    def exchange(values):
        return lax.all_to_all(values, "expert", 0, 0, tiled=True, axis_index_groups=same_core)

    def exchange_seq(values):
        return lax.all_to_all(values, "seq", 0, 0, tiled=True, axis_index_groups=[seq_order])

    tokens_other, cotangent_other = swap(tokens), swap(cotangent)
    (message,) = call(copies_kernel, [((half, rows, width), BF16)], slot_keys)
    keys, logits, columns, tokens_both = call(
        logit_kernel,
        [((own, width), BF16), ((own, both), F32), ((2, both), F32), ((both, width), BF16)],
        exchange(message), tokens, tokens_other,
    )
    columns_other = swap(columns)
    sums, stats, cotangent_both = call(
        dispatch_kernel,
        [((half, rows, width), BF16), ((half, rows, TAIL), BF16), ((both, width), BF16)],
        logits, tokens_both, cotangent, cotangent_other,
    )
    combine, message = call(
        combine_kernel,
        [((own, both), BF16), ((half, rows, long), BF16)],
        logits, columns, columns_other, cotangent_both, sums, stats,
    )
    (message,) = call(merge_kernel, [((seq, rows, long), BF16)], exchange(message))
    parts, sums, stats, slot_in, out_grad, hidden, pre_grad = call(
        expert_kernel,
        [
            ((seq, rows, 2 * width), BF16),
            ((rows, width), F32),
            ((rows, 128), F32),
            ((rows, width), BF16),
            ((rows, width), BF16),
            ((rows, hidden_units), BF16),
            ((rows, hidden_units), BF16),
        ],
        exchange_seq(message), w_in[0], w_out[0],
    )
    (message,) = call(
        outs_kernel, [((half, rows, long), BF16)], exchange_seq(parts), sums, stats
    )
    outs = exchange(message)
    dots, columns = call(
        combine_dot_kernel,
        [((own, both), F32), ((2, both), F32)],
        outs, cotangent_both, combine,
    )
    columns_other = swap(columns)
    dispatch, term = call(
        pick_kernel,
        [((own, both), BF16), ((own, both), F32)],
        outs, tokens_both, logits,
    )
    message, logit_grad = call(
        key_kernel,
        [((half, rows, width), BF16), ((own, both), BF16)],
        term, dots, combine, columns, columns_other, tokens_both,
    )
    message = exchange(message)
    pack, weights = call(
        pack_kernel,
        [((own, 3 * width + 3 * count), BF16), ((own, 3 * count), BF16)],
        outs, keys, combine, dispatch, logit_grad,
    )
    factors = (slot_in, out_grad, hidden, pre_grad)
    slot_out, rest, combine, rest_weights, slot_in, out_grad, hidden, pre_grad = call(
        token_kernel,
        [
            ((2 * own, width), BF16),
            ((4 * own, width), BF16),
            ((2 * own, count), BF16),
            ((4 * own, count), BF16),
        ]
        + [(v.shape, v.dtype) for v in factors],
        pack, swap(pack), weights, *factors,
    )
    layer_out = dot(combine, slot_out, 0, 0).astype(BF16)
    token_grad = dot(rest_weights, rest, 0, 0).astype(BF16)
    w_out_grad = dot(hidden, out_grad, 0, 0).astype(BF16)[None]
    w_in_grad = dot(slot_in, pre_grad, 0, 0).astype(BF16)[None]
    results = (layer_out, token_grad, w_in_grad, w_out_grad)
    (message,) = call(
        key_merge_kernel, [((seq, rows, width), BF16)], message, *results, far=(1, 2, 3, 4)
    )
    (key_grad,) = call(key_sum_kernel, [((rows, width), F32)], exchange_seq(message), vmem=False)

    return (layer_out, token_grad, key_grad, w_in_grad, w_out_grad)


def solution(mesh):
    in_specs = (
        P(("seq", "expert"), None),
        P("expert", None),
        P("expert", None, "seq"),
        P("expert", "seq", None),
        P(("seq", "expert"), None),
    )
    out_specs = (
        P(("seq", "expert"), None),
        P(("seq", "expert"), None),
        P("expert", None),
        P("expert", None, "seq"),
        P("expert", "seq", None),
    )
    return jax.shard_map(body, mesh=mesh, in_specs=in_specs, out_specs=out_specs, check_vma=False)
```

```python
import math

import jax
import jax.numpy as jnp
from jax import lax
from jax.experimental import pallas as pl
from jax.experimental.pallas import tpu as pltpu
from jax.sharding import PartitionSpec as P

F32 = jnp.float32
BF16 = jnp.bfloat16
TAIL = 128
ROOT = math.sqrt(2.0 / math.pi)
CUBE = 0.044715


def dot(a, b, a_dim, b_dim):
    return lax.dot_general(a, b, (((a_dim,), (b_dim,)), ((), ())), preferred_element_type=F32)


def pieces(values):
    high = values.astype(BF16).astype(F32)
    rest = values - high
    middle = rest.astype(BF16).astype(F32)
    return [high, middle, rest - middle]


def stat_block(stats):
    lane = lax.broadcasted_iota(jnp.int32, (stats[0].shape[0], TAIL), 1)
    block = jnp.zeros(lane.shape, F32)
    for i, piece in enumerate([p for s in stats for p in pieces(s)]):
        block = jnp.where(lane == i, piece, block)
    return block


def read_stat(block, i):
    cols = [block[..., k : k + 1].astype(F32) for k in range(3 * i, 3 * i + 3)]
    return cols[0] + cols[1] + cols[2]


def copies_kernel(values, out):
    for i in range(out.shape[0]):
        out[i] = values[...]


def logit_kernel(message, tokens, tokens_other, keys, logits, columns, tokens_both):
    own, width = keys.shape
    count = tokens.shape[0]
    keys[...] = message[...].reshape(own, width)
    tokens_both[:count] = tokens[...]
    tokens_both[count:] = tokens_other[...]
    value = dot(keys[...], tokens_both[...], 1, 1)
    logits[...] = value
    peak = jnp.max(value, axis=0, keepdims=True)
    columns[0:1, :] = peak
    columns[1:2, :] = jnp.sum(jnp.exp(value - peak), axis=0, keepdims=True)


def dispatch_kernel(logits, tokens_both, cotangent, cotangent_other, sums, stats, cotangent_both):
    count = cotangent.shape[0]
    cotangent_both[:count] = cotangent[...]
    cotangent_both[count:] = cotangent_other[...]
    value = logits[...]
    peak = jnp.max(value, axis=1, keepdims=True)
    weights = jnp.exp(value - peak)
    total = jnp.sum(weights, axis=1, keepdims=True)
    part = dot(weights.astype(BF16), tokens_both[...], 1, 0)
    sums[...] = part.astype(BF16).reshape(sums.shape)
    stats[...] = stat_block([peak, total]).astype(BF16).reshape(stats.shape)


def turn(columns, count):
    return jnp.concatenate([columns[:, count:], columns[:, :count]], axis=1)


def combine_kernel(logits, columns, columns_other, cotangent_both, sums, stats, combine, out):
    count, width = cotangent_both.shape[0] // 2, cotangent_both.shape[1]
    other = turn(columns_other[...], count)
    here = columns[...]
    peak = jnp.maximum(here[0:1], other[0:1])
    total = here[1:2] * jnp.exp(here[0:1] - peak) + other[1:2] * jnp.exp(other[0:1] - peak)
    weights = (jnp.exp(logits[...] - peak) / total).astype(BF16)
    combine[...] = weights
    part = dot(weights, cotangent_both[...], 1, 0)
    out[:, :, :width] = sums[...]
    out[:, :, width : 2 * width] = part.astype(BF16).reshape(sums.shape)
    out[:, :, 2 * width :] = stats[...]


def merge(message):
    width = (message.shape[2] - TAIL) // 2
    stats = message[:, :, 2 * width : 2 * width + 128]
    peaks, totals = read_stat(stats, 0), read_stat(stats, 1)
    top = jnp.max(peaks, axis=0, keepdims=True)
    scales = jnp.exp(peaks - top)
    total = jnp.sum(totals * scales, axis=0)
    first = message[0, :, :width].astype(F32) * scales[0]
    for p in range(1, message.shape[0]):
        first += message[p, :, :width].astype(F32) * scales[p]
    second = message[0, :, width : 2 * width].astype(F32)
    for p in range(1, message.shape[0]):
        second += message[p, :, width : 2 * width].astype(F32)
    return first, second, top[0], total


def merge_kernel(message, out):
    width = (message.shape[2] - TAIL) // 2
    first, second, top, total = merge(message)
    first, second = first.astype(BF16), second.astype(BF16)
    block = stat_block([top, total]).astype(BF16)
    for i in range(out.shape[0]):
        out[i, :, :width] = first
        out[i, :, width : 2 * width] = second
        out[i, :, 2 * width :] = block


def expert_kernel(
    message, w_in, w_out, parts, sums, stats, slot_in_out, out_grad_out, hidden_out, pre_grad_out
):
    width = sums.shape[1]
    first, second, top, total = merge(message)
    slot_sum = first / total
    sums[...] = slot_sum
    lane = lax.broadcasted_iota(jnp.int32, stats.shape, 1)
    stats[...] = jnp.where(lane == 0, top, total)
    slot_in = slot_sum.astype(BF16)
    out_grad = second.astype(BF16)
    slot_in_out[...] = slot_in
    out_grad_out[...] = out_grad
    pre_act = dot(slot_in, w_in[...], 1, 0)
    tanh = jnp.tanh(ROOT * (pre_act + CUBE * (pre_act * pre_act * pre_act)))
    hidden = (pre_act * (0.5 * (1.0 + tanh))).astype(BF16)
    hidden_out[...] = hidden
    act_grad = dot(out_grad, w_out[...], 1, 1)
    slope = 0.5 * (1.0 + tanh) + 0.5 * pre_act * (1.0 - tanh * tanh) * (
        ROOT * (1.0 + 3.0 * CUBE * (pre_act * pre_act))
    )
    pre_grad = (act_grad * slope).astype(BF16)
    pre_grad_out[...] = pre_grad
    out_part = dot(hidden, w_out[...], 1, 0).astype(BF16)
    slot_part = dot(pre_grad, w_in[...], 1, 1).astype(BF16)
    for i in range(parts.shape[0]):
        parts[i, :, :width] = out_part
        parts[i, :, width:] = slot_part


def outs_kernel(parts, sums, stats, out):
    width = sums.shape[1]
    total = parts[0].astype(F32)
    for p in range(1, parts.shape[0]):
        total += parts[p].astype(F32)
    values = total.astype(BF16)
    crossing = jnp.sum(values[:, width:].astype(F32) * sums[...], axis=1, keepdims=True)
    block = stat_block([stats[:, 0:1], stats[:, 1:2], crossing]).astype(BF16)
    for i in range(out.shape[0]):
        out[i, :, : 2 * width] = values
        out[i, :, 2 * width :] = block


def combine_dot_kernel(outs, cotangent_both, combine, dots, columns):
    width = cotangent_both.shape[1]
    slot_out = outs[:, :, :width].reshape(combine.shape[0], width)
    value = dot(slot_out, cotangent_both[...], 1, 1)
    dots[...] = value
    part = jnp.sum(combine[...].astype(F32) * value, axis=0, keepdims=True)
    columns[...] = jnp.concatenate([part, part], axis=0)


def pick_kernel(outs, tokens_both, logits, dispatch, term):
    own, width = logits.shape[0], tokens_both.shape[1]
    block = outs[:, :, 2 * width : 2 * width + 128].reshape(own, 128).astype(F32)
    peak, total, crossing = (read_stat(block, i) for i in range(3))
    weights = (jnp.exp(logits[...] - peak) / total).astype(BF16)
    dispatch[...] = weights
    slot_grad = outs[:, :, width : 2 * width].reshape(own, width)
    value = dot(slot_grad, tokens_both[...], 1, 1)
    term[...] = weights.astype(F32) * (value - crossing)


def key_kernel(
    term, dots, combine, columns, columns_other, tokens_both, out, logit_grad_out
):
    count = tokens_both.shape[0] // 2
    column = columns[0:1, :] + turn(columns_other[...], count)[0:1]
    combine_grad = combine[...].astype(F32) * (dots[...] - column)
    logit_grad = (term[...] + combine_grad).astype(BF16)
    part = dot(logit_grad, tokens_both[...], 1, 0)
    out[...] = part.astype(BF16).reshape(out.shape)
    logit_grad_out[...] = logit_grad


def pack_kernel(outs, keys, combine, dispatch, logit_grad, pack, weights):
    own, width = keys.shape
    count = weights.shape[1] // 3
    pack[:, :width] = outs[:, :, :width].reshape(own, width)
    pack[:, width : 2 * width] = outs[:, :, width : 2 * width].reshape(own, width)
    pack[:, 2 * width : 3 * width] = keys[...]
    for i, values in enumerate((combine[...], dispatch[...], logit_grad[...])):
        pack[:, 3 * width + i * count : 3 * width + (i + 1) * count] = values[:, count:]
        weights[:, i * count : (i + 1) * count] = values[:, :count]


def token_kernel(pack, pack_other, weights, *refs):
    slot_out, rest, combine, rest_weights = refs[4:8]
    for here, there in zip(refs[:4], refs[8:]):
        there[...] = here[...]
    own = pack.shape[0]
    width = slot_out.shape[1]
    count = combine.shape[1]
    other = pack_other[:, 3 * width :]
    slot_out[:own] = pack[:, :width]
    slot_out[own:] = pack_other[:, :width]
    combine[:own] = weights[:, :count]
    combine[own:] = other[:, :count]
    for i in range(2):
        cols = slice((i + 1) * width, (i + 2) * width)
        rest[2 * i * own : (2 * i + 1) * own] = pack[:, cols]
        rest[(2 * i + 1) * own : (2 * i + 2) * own] = pack_other[:, cols]
        cols = slice((i + 1) * count, (i + 2) * count)
        rest_weights[2 * i * own : (2 * i + 1) * own] = weights[:, cols]
        rest_weights[(2 * i + 1) * own : (2 * i + 2) * own] = other[:, cols]


def key_merge_kernel(message, *refs):
    out = refs[-1]
    total = message[0].astype(F32)
    for p in range(1, message.shape[0]):
        total += message[p].astype(F32)
    for i in range(out.shape[0]):
        out[i] = total.astype(out.dtype)


def key_sum_kernel(message, out):
    total = message[0].astype(F32)
    for p in range(1, message.shape[0]):
        total += message[p].astype(F32)
    out[...] = total


def call(kernel, outs, *args, vmem=True, far=()):
    whole = pl.BlockSpec(memory_space=pltpu.VMEM)
    there = pl.BlockSpec(memory_space=pltpu.HBM)
    make = pltpu.VMEM if vmem else jax.ShapeDtypeStruct
    args = [
        pltpu.with_memory_space_constraint(a, pltpu.HBM) if i in far else a
        for i, a in enumerate(args)
    ]
    return pl.pallas_call(
        kernel,
        out_shape=[make(shape, dtype) for shape, dtype in outs],
        in_specs=[there if i in far else whole for i in range(len(args))],
        out_specs=[whole] * len(outs),
        compiler_params=pltpu.CompilerParams(vmem_limit_bytes=24 * 1024 * 1024),
    )(*args)


def body(tokens, slot_keys, w_in, w_out, cotangent):
    count, width = tokens.shape
    hidden_units = w_in.shape[2]
    seq = lax.axis_size("seq")
    experts = lax.axis_size("expert")
    rows = slot_keys.shape[0]
    half = experts // 2
    own = half * rows
    both = 2 * count
    long = 2 * width + TAIL
    order = [4 * i + 2 * j for j in (1, 0) for i in (4, 6, 2, 5, 7, 3, 1, 0)]
    seq_order = [6, 7, 2, 3, 5, 1, 4, 0]
    same_core = [[i + c for i in order] for c in range(2)]
    partner = [(i, i ^ 1) for i in range(experts)]

    def swap(values):
        return lax.ppermute(values, "expert", partner)

    def exchange(values):
        return lax.all_to_all(values, "expert", 0, 0, tiled=True, axis_index_groups=same_core)

    def exchange_seq(values):
        return lax.all_to_all(values, "seq", 0, 0, tiled=True, axis_index_groups=[seq_order])

    tokens_other, cotangent_other = swap(tokens), swap(cotangent)
    (message,) = call(copies_kernel, [((half, rows, width), BF16)], slot_keys)
    keys, logits, columns, tokens_both = call(
        logit_kernel,
        [((own, width), BF16), ((own, both), F32), ((2, both), F32), ((both, width), BF16)],
        exchange(message), tokens, tokens_other,
    )
    columns_other = swap(columns)
    sums, stats, cotangent_both = call(
        dispatch_kernel,
        [((half, rows, width), BF16), ((half, rows, TAIL), BF16), ((both, width), BF16)],
        logits, tokens_both, cotangent, cotangent_other,
    )
    combine, message = call(
        combine_kernel,
        [((own, both), BF16), ((half, rows, long), BF16)],
        logits, columns, columns_other, cotangent_both, sums, stats,
    )
    (message,) = call(merge_kernel, [((seq, rows, long), BF16)], exchange(message))
    parts, sums, stats, slot_in, out_grad, hidden, pre_grad = call(
        expert_kernel,
        [
            ((seq, rows, 2 * width), BF16),
            ((rows, width), F32),
            ((rows, 128), F32),
            ((rows, width), BF16),
            ((rows, width), BF16),
            ((rows, hidden_units), BF16),
            ((rows, hidden_units), BF16),
        ],
        exchange_seq(message), w_in[0], w_out[0],
    )
    (message,) = call(
        outs_kernel, [((half, rows, long), BF16)], exchange_seq(parts), sums, stats
    )
    outs = exchange(message)
    dots, columns = call(
        combine_dot_kernel,
        [((own, both), F32), ((2, both), F32)],
        outs, cotangent_both, combine,
    )
    columns_other = swap(columns)
    dispatch, term = call(
        pick_kernel,
        [((own, both), BF16), ((own, both), F32)],
        outs, tokens_both, logits,
    )
    message, logit_grad = call(
        key_kernel,
        [((half, rows, width), BF16), ((own, both), BF16)],
        term, dots, combine, columns, columns_other, tokens_both,
    )
    message = exchange(message)
    pack, weights = call(
        pack_kernel,
        [((own, 3 * width + 3 * count), BF16), ((own, 3 * count), BF16)],
        outs, keys, combine, dispatch, logit_grad,
    )
    factors = (slot_in, out_grad, hidden, pre_grad)
    slot_out, rest, combine, rest_weights, slot_in, out_grad, hidden, pre_grad = call(
        token_kernel,
        [
            ((2 * own, width), BF16),
            ((4 * own, width), BF16),
            ((2 * own, count), BF16),
            ((4 * own, count), BF16),
        ]
        + [(v.shape, v.dtype) for v in factors],
        pack, swap(pack), weights, *factors,
    )
    layer_out = dot(combine, slot_out, 0, 0).astype(BF16)
    token_grad = dot(rest_weights, rest, 0, 0).astype(BF16)
    w_out_grad = dot(hidden, out_grad, 0, 0).astype(BF16)[None]
    w_in_grad = dot(slot_in, pre_grad, 0, 0).astype(BF16)[None]
    results = (layer_out, token_grad, w_in_grad, w_out_grad)
    (message,) = call(
        key_merge_kernel, [((seq, rows, width), BF16)], message, *results, far=(1, 2, 3, 4)
    )
    (key_grad,) = call(key_sum_kernel, [((rows, width), F32)], exchange_seq(message), vmem=False)

    return (layer_out, token_grad, key_grad, w_in_grad, w_out_grad)


def solution(mesh):
    in_specs = (
        P(("seq", "expert"), None),
        P("expert", None),
        P("expert", None, "seq"),
        P("expert", "seq", None),
        P(("seq", "expert"), None),
    )
    out_specs = (
        P(("seq", "expert"), None),
        P(("seq", "expert"), None),
        P("expert", None),
        P("expert", None, "seq"),
        P("expert", "seq", None),
    )
    return jax.shard_map(body, mesh=mesh, in_specs=in_specs, out_specs=out_specs, check_vma=False)
```

```python
import math

import jax
import jax.numpy as jnp
from jax import lax
from jax.experimental import pallas as pl
from jax.experimental.pallas import tpu as pltpu
from jax.sharding import PartitionSpec as P

F32 = jnp.float32
BF16 = jnp.bfloat16
TAIL = 128
ROOT = math.sqrt(2.0 / math.pi)
CUBE = 0.044715


def dot(a, b, a_dim, b_dim):
    return lax.dot_general(a, b, (((a_dim,), (b_dim,)), ((), ())), preferred_element_type=F32)


def pieces(values):
    high = values.astype(BF16).astype(F32)
    rest = values - high
    middle = rest.astype(BF16).astype(F32)
    return [high, middle, rest - middle]


def stat_block(stats):
    lane = lax.broadcasted_iota(jnp.int32, (stats[0].shape[0], TAIL), 1)
    block = jnp.zeros(lane.shape, F32)
    for i, piece in enumerate([p for s in stats for p in pieces(s)]):
        block = jnp.where(lane == i, piece, block)
    return block


def read_stat(block, i):
    cols = [block[..., k : k + 1].astype(F32) for k in range(3 * i, 3 * i + 3)]
    return cols[0] + cols[1] + cols[2]


def copies_kernel(values, out):
    for i in range(out.shape[0]):
        out[i] = values[...]


def logit_kernel(message, tokens, tokens_other, keys, logits, columns, tokens_both):
    own, width = keys.shape
    count = tokens.shape[0]
    keys[...] = message[...].reshape(own, width)
    tokens_both[:count] = tokens[...]
    tokens_both[count:] = tokens_other[...]
    value = dot(keys[...], tokens_both[...], 1, 1)
    logits[...] = value
    peak = jnp.max(value, axis=0, keepdims=True)
    columns[0:1, :] = peak
    columns[1:2, :] = jnp.sum(jnp.exp(value - peak), axis=0, keepdims=True)


def dispatch_kernel(logits, tokens_both, cotangent, cotangent_other, sums, stats, cotangent_both):
    count = cotangent.shape[0]
    cotangent_both[:count] = cotangent[...]
    cotangent_both[count:] = cotangent_other[...]
    value = logits[...]
    peak = jnp.max(value, axis=1, keepdims=True)
    weights = jnp.exp(value - peak)
    total = jnp.sum(weights, axis=1, keepdims=True)
    part = dot(weights.astype(BF16), tokens_both[...], 1, 0)
    sums[...] = part.astype(BF16).reshape(sums.shape)
    stats[...] = stat_block([peak, total]).astype(BF16).reshape(stats.shape)


def turn(columns, count):
    return jnp.concatenate([columns[:, count:], columns[:, :count]], axis=1)


def combine_kernel(logits, columns, columns_other, cotangent_both, sums, stats, combine, out):
    count, width = cotangent_both.shape[0] // 2, cotangent_both.shape[1]
    other = turn(columns_other[...], count)
    here = columns[...]
    peak = jnp.maximum(here[0:1], other[0:1])
    total = here[1:2] * jnp.exp(here[0:1] - peak) + other[1:2] * jnp.exp(other[0:1] - peak)
    weights = (jnp.exp(logits[...] - peak) / total).astype(BF16)
    combine[...] = weights
    part = dot(weights, cotangent_both[...], 1, 0)
    out[:, :, :width] = sums[...]
    out[:, :, width : 2 * width] = part.astype(BF16).reshape(sums.shape)
    out[:, :, 2 * width :] = stats[...]


def merge(message):
    width = (message.shape[2] - TAIL) // 2
    stats = message[:, :, 2 * width : 2 * width + 128]
    peaks, totals = read_stat(stats, 0), read_stat(stats, 1)
    top = jnp.max(peaks, axis=0, keepdims=True)
    scales = jnp.exp(peaks - top)
    total = jnp.sum(totals * scales, axis=0)
    first = message[0, :, :width].astype(F32) * scales[0]
    for p in range(1, message.shape[0]):
        first += message[p, :, :width].astype(F32) * scales[p]
    second = message[0, :, width : 2 * width].astype(F32)
    for p in range(1, message.shape[0]):
        second += message[p, :, width : 2 * width].astype(F32)
    return first, second, top[0], total


def merge_kernel(message, out):
    width = (message.shape[2] - TAIL) // 2
    first, second, top, total = merge(message)
    first, second = first.astype(BF16), second.astype(BF16)
    block = stat_block([top, total]).astype(BF16)
    for i in range(out.shape[0]):
        out[i, :, :width] = first
        out[i, :, width : 2 * width] = second
        out[i, :, 2 * width :] = block


def expert_kernel(
    message, w_in, w_out, parts, sums, stats, slot_in_out, out_grad_out, hidden_out, pre_grad_out
):
    width = sums.shape[1]
    first, second, top, total = merge(message)
    slot_sum = first / total
    sums[...] = slot_sum
    lane = lax.broadcasted_iota(jnp.int32, stats.shape, 1)
    stats[...] = jnp.where(lane == 0, top, total)
    slot_in = slot_sum.astype(BF16)
    out_grad = second.astype(BF16)
    slot_in_out[...] = slot_in
    out_grad_out[...] = out_grad
    pre_act = dot(slot_in, w_in[...], 1, 0)
    tanh = jnp.tanh(ROOT * (pre_act + CUBE * (pre_act * pre_act * pre_act)))
    hidden = (pre_act * (0.5 * (1.0 + tanh))).astype(BF16)
    hidden_out[...] = hidden
    act_grad = dot(out_grad, w_out[...], 1, 1)
    slope = 0.5 * (1.0 + tanh) + 0.5 * pre_act * (1.0 - tanh * tanh) * (
        ROOT * (1.0 + 3.0 * CUBE * (pre_act * pre_act))
    )
    pre_grad = (act_grad * slope).astype(BF16)
    pre_grad_out[...] = pre_grad
    out_part = dot(hidden, w_out[...], 1, 0).astype(BF16)
    slot_part = dot(pre_grad, w_in[...], 1, 1).astype(BF16)
    for i in range(parts.shape[0]):
        parts[i, :, :width] = out_part
        parts[i, :, width:] = slot_part


def outs_kernel(parts, sums, stats, out):
    width = sums.shape[1]
    total = parts[0].astype(F32)
    for p in range(1, parts.shape[0]):
        total += parts[p].astype(F32)
    values = total.astype(BF16)
    crossing = jnp.sum(values[:, width:].astype(F32) * sums[...], axis=1, keepdims=True)
    block = stat_block([stats[:, 0:1], stats[:, 1:2], crossing]).astype(BF16)
    for i in range(out.shape[0]):
        out[i, :, : 2 * width] = values
        out[i, :, 2 * width :] = block


def combine_dot_kernel(outs, cotangent_both, combine, dots, columns):
    width = cotangent_both.shape[1]
    slot_out = outs[:, :, :width].reshape(combine.shape[0], width)
    value = dot(slot_out, cotangent_both[...], 1, 1)
    dots[...] = value
    part = jnp.sum(combine[...].astype(F32) * value, axis=0, keepdims=True)
    columns[...] = jnp.concatenate([part, part], axis=0)


def pick_kernel(outs, tokens_both, logits, dispatch, term):
    own, width = logits.shape[0], tokens_both.shape[1]
    block = outs[:, :, 2 * width : 2 * width + 128].reshape(own, 128).astype(F32)
    peak, total, crossing = (read_stat(block, i) for i in range(3))
    weights = (jnp.exp(logits[...] - peak) / total).astype(BF16)
    dispatch[...] = weights
    slot_grad = outs[:, :, width : 2 * width].reshape(own, width)
    value = dot(slot_grad, tokens_both[...], 1, 1)
    term[...] = weights.astype(F32) * (value - crossing)


def key_kernel(
    term, dots, combine, columns, columns_other, tokens_both, out, logit_grad_out
):
    count = tokens_both.shape[0] // 2
    column = columns[0:1, :] + turn(columns_other[...], count)[0:1]
    combine_grad = combine[...].astype(F32) * (dots[...] - column)
    logit_grad = (term[...] + combine_grad).astype(BF16)
    part = dot(logit_grad, tokens_both[...], 1, 0)
    out[...] = part.astype(BF16).reshape(out.shape)
    logit_grad_out[...] = logit_grad


def pack_kernel(outs, keys, combine, dispatch, logit_grad, pack, weights):
    own, width = keys.shape
    count = weights.shape[1] // 3
    pack[:, :width] = outs[:, :, :width].reshape(own, width)
    pack[:, width : 2 * width] = outs[:, :, width : 2 * width].reshape(own, width)
    pack[:, 2 * width : 3 * width] = keys[...]
    for i, values in enumerate((combine[...], dispatch[...], logit_grad[...])):
        pack[:, 3 * width + i * count : 3 * width + (i + 1) * count] = values[:, count:]
        weights[:, i * count : (i + 1) * count] = values[:, :count]


def token_kernel(pack, pack_other, weights, *refs):
    slot_out, rest, combine, rest_weights = refs[4:8]
    for here, there in zip(refs[:4], refs[8:]):
        there[...] = here[...]
    own = pack.shape[0]
    width = slot_out.shape[1]
    count = combine.shape[1]
    other = pack_other[:, 3 * width :]
    slot_out[:own] = pack[:, :width]
    slot_out[own:] = pack_other[:, :width]
    combine[:own] = weights[:, :count]
    combine[own:] = other[:, :count]
    for i in range(2):
        cols = slice((i + 1) * width, (i + 2) * width)
        rest[2 * i * own : (2 * i + 1) * own] = pack[:, cols]
        rest[(2 * i + 1) * own : (2 * i + 2) * own] = pack_other[:, cols]
        cols = slice((i + 1) * count, (i + 2) * count)
        rest_weights[2 * i * own : (2 * i + 1) * own] = weights[:, cols]
        rest_weights[(2 * i + 1) * own : (2 * i + 2) * own] = other[:, cols]


def key_merge_kernel(message, *refs):
    out = refs[-1]
    total = message[0].astype(F32)
    for p in range(1, message.shape[0]):
        total += message[p].astype(F32)
    for i in range(out.shape[0]):
        out[i] = total.astype(out.dtype)


def key_sum_kernel(message, out):
    total = message[0].astype(F32)
    for p in range(1, message.shape[0]):
        total += message[p].astype(F32)
    out[...] = total


def call(kernel, outs, *args, vmem=True, far=()):
    whole = pl.BlockSpec(memory_space=pltpu.VMEM)
    there = pl.BlockSpec(memory_space=pltpu.HBM)
    make = pltpu.VMEM if vmem else jax.ShapeDtypeStruct
    args = [
        pltpu.with_memory_space_constraint(a, pltpu.HBM) if i in far else a
        for i, a in enumerate(args)
    ]
    return pl.pallas_call(
        kernel,
        out_shape=[make(shape, dtype) for shape, dtype in outs],
        in_specs=[there if i in far else whole for i in range(len(args))],
        out_specs=[whole] * len(outs),
        compiler_params=pltpu.CompilerParams(vmem_limit_bytes=24 * 1024 * 1024),
    )(*args)


def weight_kernel(slot_in, pre_grad, hidden, out_grad, w_in_grad, w_out_grad):
    w_in_grad[0] = dot(slot_in[...], pre_grad[...], 0, 0).astype(BF16)
    w_out_grad[0] = dot(hidden[...], out_grad[...], 0, 0).astype(BF16)


def weight_grads(slot_in, pre_grad, hidden, out_grad):
    rows, width = slot_in.shape
    units = hidden.shape[1]
    steps = 4
    return pl.pallas_call(
        weight_kernel,
        grid=(steps,),
        out_shape=[
            jax.ShapeDtypeStruct((1, width, units), BF16),
            jax.ShapeDtypeStruct((1, units, width), BF16),
        ],
        in_specs=[
            pl.BlockSpec((rows, width // steps), lambda i: (0, i)),
            pl.BlockSpec((rows, units), lambda i: (0, 0)),
            pl.BlockSpec((rows, units), lambda i: (0, 0)),
            pl.BlockSpec((rows, width // steps), lambda i: (0, i)),
        ],
        out_specs=[
            pl.BlockSpec((1, width // steps, units), lambda i: (0, i, 0)),
            pl.BlockSpec((1, units, width // steps), lambda i: (0, 0, i)),
        ],
        compiler_params=pltpu.CompilerParams(vmem_limit_bytes=16 * 1024 * 1024),
        cost_estimate=pl.CostEstimate(
            flops=4 * rows * width * units, bytes_accessed=4 * width * units, transcendentals=0
        ),
    )(slot_in, pre_grad, hidden, out_grad)


def body(tokens, slot_keys, w_in, w_out, cotangent):
    count, width = tokens.shape
    hidden_units = w_in.shape[2]
    seq = lax.axis_size("seq")
    experts = lax.axis_size("expert")
    rows = slot_keys.shape[0]
    half = experts // 2
    own = half * rows
    both = 2 * count
    long = 2 * width + TAIL
    order = [4 * i + 2 * j for j in (1, 0) for i in (4, 6, 2, 5, 7, 3, 1, 0)]
    seq_order = [6, 7, 2, 3, 5, 1, 4, 0]
    same_core = [[i + c for i in order] for c in range(2)]
    partner = [(i, i ^ 1) for i in range(experts)]

    def swap(values):
        return lax.ppermute(values, "expert", partner)

    def exchange(values):
        return lax.all_to_all(values, "expert", 0, 0, tiled=True, axis_index_groups=same_core)

    def exchange_seq(values):
        return lax.all_to_all(values, "seq", 0, 0, tiled=True, axis_index_groups=[seq_order])

    tokens_other, cotangent_other = swap(tokens), swap(cotangent)
    (message,) = call(copies_kernel, [((half, rows, width), BF16)], slot_keys)
    keys, logits, columns, tokens_both = call(
        logit_kernel,
        [((own, width), BF16), ((own, both), F32), ((2, both), F32), ((both, width), BF16)],
        exchange(message), tokens, tokens_other,
    )
    columns_other = swap(columns)
    sums, stats, cotangent_both = call(
        dispatch_kernel,
        [((half, rows, width), BF16), ((half, rows, TAIL), BF16), ((both, width), BF16)],
        logits, tokens_both, cotangent, cotangent_other,
    )
    combine, message = call(
        combine_kernel,
        [((own, both), BF16), ((half, rows, long), BF16)],
        logits, columns, columns_other, cotangent_both, sums, stats,
    )
    (message,) = call(merge_kernel, [((seq, rows, long), BF16)], exchange(message))
    parts, sums, stats, slot_in, out_grad, hidden, pre_grad = call(
        expert_kernel,
        [
            ((seq, rows, 2 * width), BF16),
            ((rows, width), F32),
            ((rows, 128), F32),
            ((rows, width), BF16),
            ((rows, width), BF16),
            ((rows, hidden_units), BF16),
            ((rows, hidden_units), BF16),
        ],
        exchange_seq(message), w_in[0], w_out[0],
    )
    (message,) = call(
        outs_kernel, [((half, rows, long), BF16)], exchange_seq(parts), sums, stats
    )
    outs = exchange(message)
    dots, columns = call(
        combine_dot_kernel,
        [((own, both), F32), ((2, both), F32)],
        outs, cotangent_both, combine,
    )
    columns_other = swap(columns)
    dispatch, term = call(
        pick_kernel,
        [((own, both), BF16), ((own, both), F32)],
        outs, tokens_both, logits,
    )
    message, logit_grad = call(
        key_kernel,
        [((half, rows, width), BF16), ((own, both), BF16)],
        term, dots, combine, columns, columns_other, tokens_both,
    )
    message = exchange(message)
    pack, weights = call(
        pack_kernel,
        [((own, 3 * width + 3 * count), BF16), ((own, 3 * count), BF16)],
        outs, keys, combine, dispatch, logit_grad,
    )
    factors = (slot_in, out_grad, hidden, pre_grad)
    slot_out, rest, combine, rest_weights, slot_in, out_grad, hidden, pre_grad = call(
        token_kernel,
        [
            ((2 * own, width), BF16),
            ((4 * own, width), BF16),
            ((2 * own, count), BF16),
            ((4 * own, count), BF16),
        ]
        + [(v.shape, v.dtype) for v in factors],
        pack, swap(pack), weights, *factors,
    )
    layer_out = dot(combine, slot_out, 0, 0).astype(BF16)
    token_grad = dot(rest_weights, rest, 0, 0).astype(BF16)
    w_in_grad, w_out_grad = weight_grads(slot_in, pre_grad, hidden, out_grad)
    results = (layer_out, token_grad, w_in_grad, w_out_grad)
    (message,) = call(
        key_merge_kernel, [((seq, rows, width), BF16)], message, *results, far=(1, 2, 3, 4)
    )
    (key_grad,) = call(key_sum_kernel, [((rows, width), F32)], exchange_seq(message), vmem=False)

    return (layer_out, token_grad, key_grad, w_in_grad, w_out_grad)


def solution(mesh):
    in_specs = (
        P(("seq", "expert"), None),
        P("expert", None),
        P("expert", None, "seq"),
        P("expert", "seq", None),
        P(("seq", "expert"), None),
    )
    out_specs = (
        P(("seq", "expert"), None),
        P(("seq", "expert"), None),
        P("expert", None),
        P("expert", None, "seq"),
        P("expert", "seq", None),
    )
    return jax.shard_map(body, mesh=mesh, in_specs=in_specs, out_specs=out_specs, check_vma=False)
```
